512 devices in a mesh: tok: 32 (over y_lo, z), mdl: 16 (over y_hi, x, core).
Axes of the slice: x: 4, y: 8 (y_hi: 2, y_lo: 4; y = y_hi * 4 + y_lo), z: 8, core: 2. Of those that a mesh axis runs over, the one named last changes fastest.
Arguments:
- activations: bfloat16 [6144, 8192], P('tok'), may hold values from -6 to 6
- rotation: float32 [8192, 8192], P('tok', 'mdl'), may hold values from -6 to 6
- value_weight: bfloat16 [8192, 1024], P('mdl'), may hold values from -0.0625 to 0.0625
- token_code: int32 [6144], P('tok'), may hold values from 1 to 8
- channel_code: int32 [1024], replicated, may hold values from 1 to 8
Outputs:
- new_rows: float32 [256, 8192], P('tok', 'mdl')
- recon_error: float32 [6144, 1024], P('tok')
The draws below stay inside these ranges and needn't reach their ends.
All inputs are finite; a program needn't handle non-finite values.
Results may differ from the reference program's by a relative error of at most 0.004.
Values may be sent and summed in bfloat16 or wider, within the bound.
No kernel may reach another device: no remote copies, remote signals or barrier semaphores. Data moves between devices by JAX's collectives and lax.ppermute only.
A program may use at most 64 MiB of HBM per device.

```python
import math
import jax
import jax.numpy as jnp

D = 8192
C = 1024
WIN = 8
TOKENS = 6144
ROWS = 256
N_TOK = 32


def set_ends(drawn, own_key, least, largest):
    shape = drawn.shape
    place = [jax.random.randint(jax.random.fold_in(own_key, axis), (), 0, shape[axis]) for axis in range(len(shape))]
    drawn = drawn.at[tuple(place)].set(least)
    longest = shape.index(max(shape))
    place[longest] = (place[longest] + 1) % shape[longest]
    return drawn.at[tuple(place)].set(largest)


def steps_of(own_key, shape, shards, smallest, high):
    loudness = 1.0
    for position, parts in shards:
        heights = jax.random.uniform(jax.random.fold_in(jax.random.fold_in(own_key, 6), position), (parts,), jnp.float32, smallest / len(shards), high / len(shards))
        loudness = loudness * jnp.repeat(jnp.exp(heights), shape[position] // parts).reshape((-1,) + (1,) * (len(shape) - 1 - position))
    return loudness


def gaussian(stream_key, shape, deviation, reach, cuts=(), kind=jnp.bfloat16):
    entries = jax.random.normal(stream_key, shape, jnp.float32) * deviation
    if len(cuts) > 0:
        entries = steps_of(stream_key, shape, cuts, -0.22, 0.18) * entries
    return jnp.clip(entries, min=-reach, max=reach).astype(kind)


def setup_inputs(seed: int = 0) -> dict:
    streams_of = jax.random.split(jax.random.key(seed), 6)
    return {
        "activations": gaussian(streams_of[0], (TOKENS, D), 1.0, 6.0, ((0, 32),)),
        "rotation": gaussian(streams_of[1], (D, D), 1.0, 6.0, ((0, 32), (1, 16)), jnp.float32),
        "value_weight": gaussian(streams_of[2], (D, C), D ** -0.5, 0.0625, ((0, 16),)),
        "token_code": set_ends(jax.random.randint(streams_of[3], (TOKENS,), 1, 9), jax.random.fold_in(streams_of[3], 1), 1, 8).astype(jnp.int32),
        "channel_code": set_ends(jax.random.randint(streams_of[4], (C,), 1, 9), jax.random.fold_in(streams_of[4], 1), 1, 8).astype(jnp.int32),
    }


STEP_GAIN = 0.4

def reference(activations, rotation, value_weight, token_code, channel_code):
    width_root = math.sqrt(D)
    rot_b = rotation.astype(jnp.bfloat16)
    rotated = jnp.dot(activations, rot_b, preferred_element_type=jnp.float32) / width_root
    act_clip = token_code.astype(jnp.float32)[:, None] * 0.5
    act_tanh = jnp.tanh(rotated / act_clip)
    quant_act = (act_clip * act_tanh).astype(jnp.bfloat16)
    turned = jnp.dot(rot_b.T, value_weight, preferred_element_type=jnp.float32) / width_root
    weight_clip = channel_code.astype(jnp.float32)[None, :] / (4.0 * width_root)
    weight_tanh = jnp.tanh(turned / weight_clip)
    quant_weight = (weight_clip * weight_tanh).astype(jnp.bfloat16)
    recon_error = jnp.dot(quant_act, quant_weight, preferred_element_type=jnp.float32) - jnp.dot(activations, value_weight, preferred_element_type=jnp.float32)
    error_bf = recon_error.astype(jnp.bfloat16)
    grad_act = (jnp.dot(error_bf, quant_weight.T, preferred_element_type=jnp.float32) * (1.0 - act_tanh * act_tanh)).astype(jnp.bfloat16)
    grad_turned = (jnp.dot(quant_act.T, error_bf, preferred_element_type=jnp.float32) * (1.0 - weight_tanh * weight_tanh)).astype(jnp.bfloat16)
    stack_a = jnp.concatenate([rotated.astype(jnp.bfloat16), turned.astype(jnp.bfloat16).T], 0)
    stack_g = jnp.concatenate([grad_act, grad_turned.T], 0)
    own_rows = rotation.reshape(N_TOK, D // N_TOK, D)[:, :WIN].reshape(ROWS, D)
    step_size = STEP_GAIN / math.sqrt(TOKENS * C)

    def cayley(mats):
        left_a = jnp.dot(mats, stack_a.T, preferred_element_type=jnp.float32).astype(jnp.bfloat16)
        left_g = jnp.dot(mats, stack_g.T, preferred_element_type=jnp.float32).astype(jnp.bfloat16)
        return jnp.dot(left_a, stack_g, preferred_element_type=jnp.float32) - jnp.dot(left_g, stack_a, preferred_element_type=jnp.float32)
    moved = own_rows - step_size * cayley(own_rows.astype(jnp.bfloat16))
    second_in = (own_rows + moved).astype(jnp.bfloat16)
    new_rows = own_rows - 0.5 * step_size * cayley(second_in)
    return (new_rows, recon_error)
```

```python
import math

import jax
import jax.numpy as jnp
from jax import lax
from jax.sharding import PartitionSpec as P

WIN = 8


STEP_GAIN = 0.4


def gather_blocks(own, axis):
    parts = lax.axis_size(axis)
    return lax.all_to_all(jnp.broadcast_to(own[None], (parts,) + own.shape), axis, 0, 0)


def sum_blocks(blocks, axis):
    return jnp.sum(lax.all_to_all(blocks, axis, 0, 0).astype(jnp.float32), 0)


def cayley_lefts(mats, stack_a, stack_g):
    rows = mats.shape[0]
    row_total = stack_a.shape[0]
    parts = lax.axis_size("mdl")
    stacked = jnp.concatenate([stack_a, stack_g], 0)
    products = jnp.einsum("rd,kd->rk", mats, stacked, preferred_element_type=jnp.float32)
    products = products.astype(jnp.bfloat16).reshape(parts, rows // parts, 2 * row_total)
    own_sum = sum_blocks(products, "mdl").astype(jnp.bfloat16)
    lefts = gather_blocks(own_sum, "mdl").reshape(rows, 2 * row_total)
    return lefts[:, :row_total], lefts[:, row_total:]


def cayley_own(mats, stack_a, stack_g):
    left_a, left_g = cayley_lefts(mats, stack_a, stack_g)
    partial = jnp.dot(left_a, stack_g, preferred_element_type=jnp.float32) - jnp.dot(
        left_g, stack_a, preferred_element_type=jnp.float32
    )
    parts = lax.axis_size("tok")
    return sum_blocks(partial.reshape(parts, -1, partial.shape[1]), "tok")


def local(activations, rotation, value_weight, token_code, channel_code):
    n_tok = lax.axis_size("tok")
    n_mdl = lax.axis_size("mdl")
    tok_pos = lax.axis_index("tok")
    mdl_pos = lax.axis_index("mdl")
    block_rows = rotation.shape[0]
    narrow = rotation.shape[1]
    model_width = activations.shape[1]
    channels = value_weight.shape[1]
    chan_share = channels // n_tok
    tok_rows = activations.shape[0]
    width_root = math.sqrt(model_width)
    rot_b = rotation.astype(jnp.bfloat16)
    rot_panel = lax.all_gather(rot_b, "tok", axis=0, tiled=True)
    own_cols = lax.dynamic_slice_in_dim(value_weight, tok_pos * chan_share, chan_share, 1)
    weight_rows = gather_blocks(own_cols.T, "mdl").transpose(1, 0, 2).reshape(chan_share, model_width)
    own_feats = lax.dynamic_slice_in_dim(activations, mdl_pos * narrow, narrow, 1)
    plain = jnp.dot(own_feats, value_weight, preferred_element_type=jnp.float32)

    turned = jnp.dot(weight_rows, rot_panel, preferred_element_type=jnp.float32) / width_root
    own_codes = lax.dynamic_slice_in_dim(channel_code, tok_pos * chan_share, chan_share, 0)
    weight_clip = own_codes.astype(jnp.float32)[:, None] / (4.0 * width_root)
    weight_tanh = jnp.tanh(turned / weight_clip)
    quant_weight = (weight_clip * weight_tanh).astype(jnp.bfloat16)
    weight_full = gather_blocks(quant_weight, "tok").reshape(channels, narrow)

    rotated = jnp.dot(activations, rot_panel, preferred_element_type=jnp.float32) / width_root
    act_clip = token_code.astype(jnp.float32)[:, None] * 0.5
    act_tanh = jnp.tanh(rotated / act_clip)
    quant_act = (act_clip * act_tanh).astype(jnp.bfloat16)
    window = rot_panel.reshape(n_tok, block_rows, narrow)[:, :WIN].reshape(n_tok * WIN, narrow)

    partial_err = (
        jnp.einsum("td,cd->tc", quant_act, weight_full, preferred_element_type=jnp.float32) - plain
    )
    lanes = channels * 2 // n_mdl
    halves = partial_err.reshape(2, tok_rows // 2, n_mdl // 2, lanes).transpose(0, 2, 1, 3)
    own_err = sum_blocks(halves.reshape(n_mdl, tok_rows // 2, lanes), "mdl")
    recon_error = gather_blocks(own_err, "mdl").reshape(2, n_mdl // 2, tok_rows // 2, lanes)
    recon_error = recon_error.transpose(0, 2, 1, 3).reshape(tok_rows, channels)
    error_bf = recon_error.astype(jnp.bfloat16)
    grad_quant = sum_blocks(
        jnp.einsum("tc,td->cd", error_bf, quant_act, preferred_element_type=jnp.float32)
        .astype(jnp.bfloat16)
        .reshape(n_tok, chan_share, narrow),
        "tok",
    )
    grad_act = (
        jnp.dot(error_bf, weight_full, preferred_element_type=jnp.float32)
        * (1.0 - act_tanh * act_tanh)
    ).astype(jnp.bfloat16)
    grad_turned = (grad_quant * (1.0 - weight_tanh * weight_tanh)).astype(jnp.bfloat16)
    stack_a = jnp.concatenate([rotated.astype(jnp.bfloat16), turned.astype(jnp.bfloat16)], 0)
    stack_g = jnp.concatenate([grad_act, grad_turned], 0)
    step_size = STEP_GAIN / math.sqrt(tok_rows * n_tok * channels)
    own_rows = rotation[:WIN]
    moved = own_rows - step_size * cayley_own(window, stack_a, stack_g)
    second_in = gather_blocks((own_rows + moved).astype(jnp.bfloat16), "tok")
    second_in = second_in.reshape(n_tok * WIN, narrow)
    new_rows = own_rows - 0.5 * step_size * cayley_own(second_in, stack_a, stack_g)
    return (new_rows, recon_error)


def solution(mesh):
    in_specs = (P("tok", None), P("tok", "mdl"), P("mdl", None), P("tok"), P())
    out_specs = (P("tok", "mdl"), P("tok", None))
    return jax.shard_map(local, mesh=mesh, in_specs=in_specs, out_specs=out_specs, check_vma=False)
```

```python
import math

import jax
import jax.numpy as jnp
from jax import lax
from jax.sharding import Mesh
from jax.sharding import PartitionSpec as P

WIN = 8


STEP_GAIN = 0.4

LINE, RING = 4, 8
TOK = ("line", "ring")
THIN = 128


def gather_blocks(own, axis):
    parts = lax.axis_size(axis)
    return lax.all_to_all(jnp.broadcast_to(own[None], (parts,) + own.shape), axis, 0, 0)


def sum_blocks(blocks, axis):
    return jnp.sum(lax.all_to_all(blocks, axis, 0, 0).astype(jnp.float32), 0)


def cayley_lefts(mats, stack_a, stack_g):
    rows = mats.shape[0]
    row_total = stack_a.shape[0]
    parts = lax.axis_size("mdl")
    stacked = jnp.concatenate([stack_a, stack_g], 0)
    products = jnp.einsum("rd,kd->rk", mats, stacked, preferred_element_type=jnp.float32)
    products = products.astype(jnp.bfloat16).reshape(parts, rows // parts, 2 * row_total)
    own_sum = sum_blocks(products, "mdl").astype(jnp.bfloat16)
    lefts = gather_blocks(own_sum, "mdl").reshape(rows, 2 * row_total)
    return lefts[:, :row_total], lefts[:, row_total:]


def cayley_own(mats, stack_a, stack_g):
    left_a, left_g = cayley_lefts(mats, stack_a, stack_g)
    partial = jnp.dot(left_a, stack_g, preferred_element_type=jnp.float32) - jnp.dot(
        left_g, stack_a, preferred_element_type=jnp.float32
    )
    parts = lax.axis_size(TOK)
    return sum_blocks(partial.reshape(parts, -1, partial.shape[1]), TOK)


def roll_blocks(blocks, start, dim):
    twice = jnp.concatenate([blocks, blocks], dim)
    return lax.dynamic_slice_in_dim(twice, start, blocks.shape[dim], dim)


def ring_pass(own, up_steps, down_steps):
    up = [(k, (k + 1) % RING) for k in range(RING)]
    down = [(k, (k - 1) % RING) for k in range(RING)]
    found = {0: own}
    for step in range(1, max(up_steps, down_steps) + 1):
        if step <= up_steps:
            found[RING - step] = lax.ppermute(found[(RING - step + 1) % RING], "ring", up)
        if step <= down_steps:
            found[step] = lax.ppermute(found[step - 1], "ring", down)
    return [found[k] for k in range(RING)]


def times_rotation(lhs_blocks, rot_b, line_pos, ring_pos):
    rows, narrow = rot_b.shape
    half = rows // 2
    wide = narrow - THIN
    count = lhs_blocks.shape[1]

    line_wide = gather_blocks(rot_b[:, THIN:], "line")
    near_lo = ring_pass(rot_b[:half], RING // 2, RING // 2 - 1)
    near_hi = ring_pass(rot_b[half:], RING // 2 - 1, RING // 2)
    others = roll_blocks(line_wide, line_pos + 1, 0)[: LINE - 1]
    far_lo = ring_pass(others[:, :half], RING // 2, RING // 2 - 1)
    far_hi = ring_pass(others[:, half:], RING // 2 - 1, RING // 2)
    ring_thin = jnp.stack(
        [jnp.concatenate([lo[:, :THIN], hi[:, :THIN]], 0) for lo, hi in zip(near_lo, near_hi)]
    )
    thin = gather_blocks(ring_thin, "line")

    grid = lhs_blocks.reshape(LINE, RING, count, rows)
    by_ring = roll_blocks(grid, ring_pos, 1)
    by_both = roll_blocks(by_ring, line_pos, 0)
    lhs_thin = by_ring.transpose(2, 0, 1, 3).reshape(count, LINE * RING * rows)
    lhs_far = by_both[1:].reshape(LINE - 1, RING, count, 2, half)
    lhs_far = lhs_far.transpose(1, 3, 2, 0, 4).reshape(RING, 2, count, (LINE - 1) * half)
    lhs_near = by_both[0].transpose(1, 0, 2).reshape(count, RING * rows)

    near = [piece[:, THIN:] for pair in zip(near_lo, near_hi) for piece in pair]
    total = jnp.dot(lhs_near, jnp.concatenate(near, 0), preferred_element_type=jnp.float32)
    for place in [0, 1, 7, 2, 6, 3, 5, 4]:
        for part, far in enumerate((far_lo, far_hi)):
            piece = far[place].reshape((LINE - 1) * half, wide)
            total = total + jnp.dot(
                lhs_far[place, part], piece, preferred_element_type=jnp.float32
            )
    total_thin = jnp.dot(
        lhs_thin, thin.reshape(LINE * RING * rows, THIN), preferred_element_type=jnp.float32
    )

    first_near = jnp.stack([piece[:WIN, THIN:] for piece in near_lo])
    first_far = jnp.stack([piece[:, :WIN] for piece in far_lo], 1)
    first = roll_blocks(
        jnp.concatenate([first_near[None], first_far], 0), (LINE - line_pos) % LINE, 0
    )
    first = jnp.concatenate([thin[:, :, :WIN], first], 3)
    first = roll_blocks(first, (RING - ring_pos) % RING, 1).reshape(LINE * RING * WIN, narrow)
    return jnp.concatenate([total_thin, total], 1), first


def local(activations, rotation, value_weight, token_code, channel_code):
    n_tok = lax.axis_size(TOK)
    n_mdl = lax.axis_size("mdl")
    tok_pos = lax.axis_index(TOK)
    mdl_pos = lax.axis_index("mdl")
    block_rows = rotation.shape[0]
    narrow = rotation.shape[1]
    model_width = activations.shape[1]
    channels = value_weight.shape[1]
    chan_share = channels // n_tok
    tok_rows = activations.shape[0]
    width_root = math.sqrt(model_width)
    rot_b = rotation.astype(jnp.bfloat16)
    own_cols = lax.dynamic_slice_in_dim(value_weight, tok_pos * chan_share, chan_share, 1)
    weight_rows = gather_blocks(own_cols.T, "mdl").reshape(n_mdl, chan_share, -1, block_rows)
    weight_rows = weight_rows.transpose(0, 2, 1, 3).reshape(n_tok, chan_share, block_rows)
    act_blocks = activations.reshape(tok_rows, n_tok, block_rows).transpose(1, 0, 2)
    products, window = times_rotation(
        jnp.concatenate([act_blocks, weight_rows], 1),
        rot_b,
        lax.axis_index("line"),
        lax.axis_index("ring"),
    )
    products = products / width_root
    rotated, turned = products[:tok_rows], products[tok_rows:]
    own_feats = lax.dynamic_slice_in_dim(activations, mdl_pos * narrow, narrow, 1)
    plain = jnp.dot(own_feats, value_weight, preferred_element_type=jnp.float32)

    own_codes = lax.dynamic_slice_in_dim(channel_code, tok_pos * chan_share, chan_share, 0)
    weight_clip = own_codes.astype(jnp.float32)[:, None] / (4.0 * width_root)
    weight_tanh = jnp.tanh(turned / weight_clip)
    quant_weight = (weight_clip * weight_tanh).astype(jnp.bfloat16)
    weight_full = gather_blocks(quant_weight, TOK).reshape(channels, narrow)

    act_clip = token_code.astype(jnp.float32)[:, None] * 0.5
    act_tanh = jnp.tanh(rotated / act_clip)
    quant_act = (act_clip * act_tanh).astype(jnp.bfloat16)
    partial_err = (
        jnp.einsum("td,cd->tc", quant_act, weight_full, preferred_element_type=jnp.float32) - plain
    )
    lanes = channels * 2 // n_mdl
    halves = partial_err.reshape(2, tok_rows // 2, n_mdl // 2, lanes).transpose(0, 2, 1, 3)
    own_err = sum_blocks(halves.reshape(n_mdl, tok_rows // 2, lanes), "mdl")
    recon_error = gather_blocks(own_err, "mdl").reshape(2, n_mdl // 2, tok_rows // 2, lanes)
    recon_error = recon_error.transpose(0, 2, 1, 3).reshape(tok_rows, channels)
    error_bf = recon_error.astype(jnp.bfloat16)
    grad_quant = sum_blocks(
        jnp.einsum("tc,td->cd", error_bf, quant_act, preferred_element_type=jnp.float32)
        .astype(jnp.bfloat16)
        .reshape(n_tok, chan_share, narrow),
        TOK,
    )
    grad_act = (
        jnp.dot(error_bf, weight_full, preferred_element_type=jnp.float32)
        * (1.0 - act_tanh * act_tanh)
    ).astype(jnp.bfloat16)
    grad_turned = (grad_quant * (1.0 - weight_tanh * weight_tanh)).astype(jnp.bfloat16)
    stack_a = products.astype(jnp.bfloat16)
    stack_g = jnp.concatenate([grad_act, grad_turned], 0)
    step_size = STEP_GAIN / math.sqrt(tok_rows * n_tok * channels)
    own_rows = rotation[:WIN]
    moved = own_rows - step_size * cayley_own(window, stack_a, stack_g)
    second_in = gather_blocks((own_rows + moved).astype(jnp.bfloat16), TOK)
    second_in = second_in.reshape(n_tok * WIN, narrow)
    new_rows = own_rows - 0.5 * step_size * cayley_own(second_in, stack_a, stack_g)
    return (new_rows, recon_error)


def solution(mesh):
    mesh = Mesh(mesh.devices.reshape(LINE, RING, -1), TOK + ("mdl",))
    in_specs = (P(TOK, None), P(TOK, "mdl"), P("mdl", None), P(TOK), P())
    out_specs = (P(TOK, "mdl"), P(TOK, None))
    return jax.shard_map(local, mesh=mesh, in_specs=in_specs, out_specs=out_specs, check_vma=False)
```

```python
import math

import jax
import jax.numpy as jnp
from jax import lax
from jax.sharding import Mesh
from jax.sharding import PartitionSpec as P

WIN = 8


STEP_GAIN = 0.4

LINE, RING = 4, 8
TOK = ("line", "ring")
THIN = 128


def gather_blocks(own, axis):
    parts = lax.axis_size(axis)
    return lax.all_to_all(jnp.broadcast_to(own[None], (parts,) + own.shape), axis, 0, 0)


def sum_blocks(blocks, axis):
    return jnp.sum(lax.all_to_all(blocks, axis, 0, 0).astype(jnp.float32), 0)


def cayley_lefts(mats, stack_a, stack_g):
    rows = mats.shape[0]
    row_total = stack_a.shape[0]
    parts = lax.axis_size("mdl")
    stacked = jnp.concatenate([stack_a, stack_g], 0)
    products = jnp.einsum("rd,kd->rk", mats, stacked, preferred_element_type=jnp.float32)
    products = products.astype(jnp.bfloat16).reshape(parts, rows // parts, 2 * row_total)
    own_sum = sum_blocks(products, "mdl").astype(jnp.bfloat16)
    lefts = gather_blocks(own_sum, "mdl").reshape(rows, 2 * row_total)
    return lefts[:, :row_total], lefts[:, row_total:]


def cayley_own(mats, stack_a, stack_g):
    left_a, left_g = cayley_lefts(mats, stack_a, stack_g)
    partial = jnp.dot(left_a, stack_g, preferred_element_type=jnp.float32) - jnp.dot(
        left_g, stack_a, preferred_element_type=jnp.float32
    )
    partial = partial.astype(jnp.bfloat16)
    parts = lax.axis_size(TOK)
    return sum_blocks(partial.reshape(parts, -1, partial.shape[1]), TOK)


def roll_blocks(blocks, start, dim):
    twice = jnp.concatenate([blocks, blocks], dim)
    return lax.dynamic_slice_in_dim(twice, start, blocks.shape[dim], dim)


def times_rotation(lhs, rot_b, line_wide, line_pos):
    rows, narrow = rot_b.shape
    wide = narrow - THIN
    count = lhs.shape[0]
    span = RING * rows

    near = lax.all_gather(rot_b, "ring", axis=0, tiled=True)
    others = roll_blocks(line_wide, line_pos + 1, 0)[: LINE - 1]
    far = lax.all_gather(others.reshape((LINE - 1) * rows, wide), "ring", axis=0, tiled=True)
    thin = gather_blocks(near[:, :THIN], "line")

    spans = jnp.stack([lhs[:, k * span : (k + 1) * span] for k in range(LINE)])
    spans = roll_blocks(spans, line_pos, 0)
    lhs_far = jnp.concatenate(
        [
            spans[1 + k, :, ring * rows : (ring + 1) * rows]
            for ring in range(RING)
            for k in range(LINE - 1)
        ],
        1,
    )
    total_thin = jnp.dot(lhs, thin.reshape(LINE * span, THIN), preferred_element_type=jnp.float32)
    total = jnp.dot(spans[0], near[:, THIN:], preferred_element_type=jnp.float32)
    total = total + jnp.dot(lhs_far, far, preferred_element_type=jnp.float32)

    first_near = near.reshape(RING, rows, narrow)[None, :, :WIN, THIN:]
    first_far = far.reshape(RING, LINE - 1, rows, wide)[:, :, :WIN].transpose(1, 0, 2, 3)
    first = jnp.concatenate([first_near, first_far], 0)
    first = roll_blocks(first, (LINE - line_pos) % LINE, 0)
    first_thin = thin.reshape(LINE, RING, rows, THIN)[:, :, :WIN]
    first = jnp.concatenate([first_thin, first], 3).reshape(LINE * RING * WIN, narrow)
    return jnp.concatenate([total_thin, total], 1), first


def local(activations, rotation, value_weight, token_code, channel_code):
    n_tok = lax.axis_size(TOK)
    n_mdl = lax.axis_size("mdl")
    tok_pos = lax.axis_index(TOK)
    mdl_pos = lax.axis_index("mdl")
    narrow = rotation.shape[1]
    model_width = activations.shape[1]
    channels = value_weight.shape[1]
    chan_share = channels // n_tok
    tok_rows = activations.shape[0]
    width_root = math.sqrt(model_width)
    rot_b = rotation.astype(jnp.bfloat16)
    line_wide = gather_blocks(rot_b[:, THIN:], "line")
    value_late, line_wide = lax.optimization_barrier((value_weight, line_wide))
    own_cols = lax.dynamic_slice_in_dim(value_late, tok_pos * chan_share, chan_share, 1)
    weight_rows = gather_blocks(own_cols.T, "mdl").transpose(1, 0, 2).reshape(chan_share, model_width)
    lhs = jnp.concatenate([activations, weight_rows], 0)
    products, window = times_rotation(lhs, rot_b, line_wide, lax.axis_index("line"))
    products = products / width_root
    rotated, turned = products[:tok_rows], products[tok_rows:]
    own_feats = lax.dynamic_slice_in_dim(activations, mdl_pos * narrow, narrow, 1)
    plain = jnp.dot(own_feats, value_weight, preferred_element_type=jnp.float32)

    own_codes = lax.dynamic_slice_in_dim(channel_code, tok_pos * chan_share, chan_share, 0)
    weight_clip = own_codes.astype(jnp.float32)[:, None] / (4.0 * width_root)
    weight_tanh = jnp.tanh(turned / weight_clip)
    quant_weight = (weight_clip * weight_tanh).astype(jnp.bfloat16)
    weight_full = gather_blocks(quant_weight, TOK).reshape(channels, narrow)

    act_clip = token_code.astype(jnp.float32)[:, None] * 0.5
    act_tanh = jnp.tanh(rotated / act_clip)
    quant_act = (act_clip * act_tanh).astype(jnp.bfloat16)
    partial_err = (
        jnp.einsum("td,cd->tc", quant_act, weight_full, preferred_element_type=jnp.float32) - plain
    )
    lanes = channels * 2 // n_mdl
    halves = partial_err.reshape(2, tok_rows // 2, n_mdl // 2, lanes).transpose(0, 2, 1, 3)
    own_err = sum_blocks(halves.reshape(n_mdl, tok_rows // 2, lanes), "mdl")
    recon_error = gather_blocks(own_err, "mdl").reshape(2, n_mdl // 2, tok_rows // 2, lanes)
    recon_error = recon_error.transpose(0, 2, 1, 3).reshape(tok_rows, channels)
    error_bf = recon_error.astype(jnp.bfloat16)
    grad_quant = sum_blocks(
        jnp.einsum("tc,td->cd", error_bf, quant_act, preferred_element_type=jnp.float32)
        .astype(jnp.bfloat16)
        .reshape(n_tok, chan_share, narrow),
        TOK,
    )
    grad_act = (
        jnp.dot(error_bf, weight_full, preferred_element_type=jnp.float32)
        * (1.0 - act_tanh * act_tanh)
    ).astype(jnp.bfloat16)
    grad_turned = (grad_quant * (1.0 - weight_tanh * weight_tanh)).astype(jnp.bfloat16)
    stack_a = products.astype(jnp.bfloat16)
    stack_g = jnp.concatenate([grad_act, grad_turned], 0)
    step_size = STEP_GAIN / math.sqrt(tok_rows * n_tok * channels)
    own_rows = rotation[:WIN]
    moved = own_rows - step_size * cayley_own(window, stack_a, stack_g)
    second_in = gather_blocks((own_rows + moved).astype(jnp.bfloat16), TOK)
    second_in = second_in.reshape(n_tok * WIN, narrow)
    new_rows = own_rows - 0.5 * step_size * cayley_own(second_in, stack_a, stack_g)
    return (new_rows, recon_error)


def solution(mesh):
    mesh = Mesh(mesh.devices.reshape(LINE, RING, -1), TOK + ("mdl",))
    in_specs = (P(TOK, None), P(TOK, "mdl"), P("mdl", None), P(TOK), P())
    out_specs = (P(TOK, "mdl"), P(TOK, None))
    return jax.shard_map(local, mesh=mesh, in_specs=in_specs, out_specs=out_specs, check_vma=False)
```

```python
import math

import jax
import jax.numpy as jnp
from jax import lax
from jax.sharding import Mesh
from jax.sharding import PartitionSpec as P

WIN = 8


STEP_GAIN = 0.4

LINE, RING = 4, 8
TOK = ("line", "ring")
MDL = ("chip", "core")
THIN = 128


def gather_blocks(own, axis):
    parts = lax.axis_size(axis)
    return lax.all_to_all(jnp.broadcast_to(own[None], (parts,) + own.shape), axis, 0, 0)


def sum_blocks(blocks, axis):
    return jnp.sum(lax.all_to_all(blocks, axis, 0, 0).astype(jnp.float32), 0)


def cayley_lefts(mats, stack_a, stack_g):
    rows = mats.shape[0]
    row_total = stack_a.shape[0]
    parts = lax.axis_size(MDL)
    stacked = jnp.concatenate([stack_a, stack_g], 0)
    products = jnp.einsum("rd,kd->rk", mats, stacked, preferred_element_type=jnp.float32)
    products = products.astype(jnp.bfloat16).reshape(parts, rows // parts, 2 * row_total)
    own_sum = lax.optimization_barrier(sum_blocks(products, MDL)).astype(jnp.bfloat16)
    lefts = gather_blocks(own_sum, MDL).reshape(rows, 2 * row_total)
    return lefts[:, :row_total], lefts[:, row_total:]


def cayley_own(mats, stack_a, stack_g):
    left_a, left_g = cayley_lefts(mats, stack_a, stack_g)
    partial = jnp.dot(left_a, stack_g, preferred_element_type=jnp.float32) - jnp.dot(
        left_g, stack_a, preferred_element_type=jnp.float32
    )
    partial = partial.astype(jnp.bfloat16)
    parts = lax.axis_size(TOK)
    return sum_blocks(partial.reshape(parts, -1, partial.shape[1]), TOK)


def times_rotation(lhs, rot_b, line_wide, line_pos):
    rows, narrow = rot_b.shape
    wide = narrow - THIN
    span = RING * rows

    def other(k, blocks):
        return jnp.where(line_pos > k, blocks[k], blocks[k + 1])

    near = lax.all_gather(rot_b, "ring", axis=0, tiled=True)
    others = jnp.stack([other(k, line_wide) for k in range(LINE - 1)])
    far = lax.all_gather(others, "ring", axis=1, tiled=True)
    thin = gather_blocks(near[:, :THIN], "line")

    spans = [lhs[:, k * span : (k + 1) * span] for k in range(LINE)]
    lhs_near = spans[LINE - 1]
    for k in range(LINE - 1):
        lhs_near = jnp.where(line_pos == k, spans[k], lhs_near)
    total_thin = jnp.dot(lhs, thin.reshape(LINE * span, THIN), preferred_element_type=jnp.float32)
    total = jnp.dot(lhs_near, near[:, THIN:], preferred_element_type=jnp.float32)
    for k in range(LINE - 1):
        total = total + jnp.dot(other(k, spans), far[k], preferred_element_type=jnp.float32)

    first_near = near.reshape(RING, rows, narrow)[:, : 2 * WIN]
    first_far = far.reshape(LINE - 1, RING, rows, wide)[:, :, : 2 * WIN]
    first_near, first_far = lax.optimization_barrier((first_near, first_far))
    first_near, first_far = first_near[:, :WIN, THIN:], first_far[:, :, :WIN]
    first = [
        jnp.where(
            line_pos == k,
            first_near,
            jnp.where(line_pos > k, first_far[min(k, LINE - 2)], first_far[max(k - 1, 0)]),
        )
        for k in range(LINE)
    ]
    first_thin = thin.reshape(LINE, RING, rows, THIN)[:, :, :WIN]
    first = jnp.concatenate([first_thin, jnp.stack(first)], 3).reshape(LINE * RING * WIN, narrow)
    return jnp.concatenate([total_thin, total], 1), first


def local(activations, rotation, value_weight, token_code, channel_code):
    n_tok = lax.axis_size(TOK)
    n_mdl = lax.axis_size(MDL)
    tok_pos = lax.axis_index(TOK)
    mdl_pos = lax.axis_index(MDL)
    narrow = rotation.shape[1]
    model_width = activations.shape[1]
    channels = value_weight.shape[1]
    chan_share = channels // n_tok
    tok_rows = activations.shape[0]
    width_root = math.sqrt(model_width)
    rot_b = rotation.astype(jnp.bfloat16)
    line_wide = gather_blocks(rot_b[:, THIN:], "line")
    value_late, line_wide = lax.optimization_barrier((value_weight, line_wide))
    own_cols = lax.dynamic_slice_in_dim(value_late, tok_pos * chan_share, chan_share, 1)
    weight_rows = gather_blocks(own_cols.T, MDL).transpose(1, 0, 2).reshape(chan_share, model_width)
    lhs = jnp.concatenate([activations, weight_rows], 0)
    products, window = times_rotation(lhs, rot_b, line_wide, lax.axis_index("line"))
    products = products / width_root
    rotated, turned = products[:tok_rows], products[tok_rows:]
    own_feats = lax.dynamic_slice_in_dim(activations, mdl_pos * narrow, narrow, 1)
    plain = jnp.dot(own_feats, value_weight, preferred_element_type=jnp.float32)

    own_codes = lax.dynamic_slice_in_dim(channel_code, tok_pos * chan_share, chan_share, 0)
    weight_clip = own_codes.astype(jnp.float32)[:, None] / (4.0 * width_root)
    weight_tanh = jnp.tanh(turned / weight_clip)
    quant_weight = (weight_clip * weight_tanh).astype(jnp.bfloat16)
    weight_full = gather_blocks(quant_weight, TOK).reshape(channels, narrow)

    act_clip = token_code.astype(jnp.float32)[:, None] * 0.5
    act_tanh = jnp.tanh(rotated / act_clip)
    quant_act = (act_clip * act_tanh).astype(jnp.bfloat16)
    partial_err = (
        jnp.einsum("td,cd->tc", quant_act, weight_full, preferred_element_type=jnp.float32) - plain
    )
    half = tok_rows // 2
    chips = lax.axis_size("chip")
    core_err = sum_blocks(partial_err.reshape(2, half, channels), "core")
    core_err = core_err.reshape(half, chips, channels // chips).transpose(1, 0, 2)
    own_err = sum_blocks(core_err, "chip")
    core_err = gather_blocks(own_err, "chip").transpose(1, 0, 2).reshape(half, channels)
    recon_error = gather_blocks(core_err, "core").reshape(tok_rows, channels)
    error_bf = recon_error.astype(jnp.bfloat16)
    grad_quant = sum_blocks(
        jnp.einsum("tc,td->cd", error_bf, quant_act, preferred_element_type=jnp.float32)
        .astype(jnp.bfloat16)
        .reshape(n_tok, chan_share, narrow),
        TOK,
    )
    grad_act = (
        jnp.dot(error_bf, weight_full, preferred_element_type=jnp.float32)
        * (1.0 - act_tanh * act_tanh)
    ).astype(jnp.bfloat16)
    grad_turned = (grad_quant * (1.0 - weight_tanh * weight_tanh)).astype(jnp.bfloat16)
    stack_a = products.astype(jnp.bfloat16)
    stack_g = jnp.concatenate([grad_act, grad_turned], 0)
    step_size = STEP_GAIN / math.sqrt(tok_rows * n_tok * channels)
    own_rows = rotation[:WIN]
    moved = own_rows - step_size * cayley_own(window, stack_a, stack_g)
    second_in = gather_blocks((own_rows + moved).astype(jnp.bfloat16), TOK)
    second_in = second_in.reshape(n_tok * WIN, narrow)
    new_rows = own_rows - 0.5 * step_size * cayley_own(second_in, stack_a, stack_g)
    return (new_rows, recon_error)


def solution(mesh):
    mesh = Mesh(mesh.devices.reshape(LINE, RING, -1, 2), TOK + MDL)
    in_specs = (P(TOK, None), P(TOK, MDL), P(MDL, None), P(TOK), P())
    out_specs = (P(TOK, MDL), P(TOK, None))
    return jax.shard_map(local, mesh=mesh, in_specs=in_specs, out_specs=out_specs, check_vma=False)
```

```python
import math

import jax
import jax.numpy as jnp
from jax import lax
from jax.sharding import Mesh
from jax.sharding import PartitionSpec as P

WIN = 8


STEP_GAIN = 0.4

LINE, RING = 4, 8
TOK = ("line", "ring")
MDL = ("chip", "core")
THIN = 128


def gather_blocks(own, axis):
    parts = lax.axis_size(axis)
    return lax.all_to_all(jnp.broadcast_to(own[None], (parts,) + own.shape), axis, 0, 0)


def sum_blocks(blocks, axis):
    return jnp.sum(lax.all_to_all(blocks, axis, 0, 0).astype(jnp.float32), 0)


def cayley_lefts(mats, stack_a, stack_g):
    rows = mats.shape[0]
    row_total = stack_a.shape[0]
    parts = lax.axis_size(MDL)
    stacked = jnp.concatenate([stack_a, stack_g], 0)
    products = jnp.einsum("rd,kd->rk", mats, stacked, preferred_element_type=jnp.float32)
    products = products.astype(jnp.bfloat16).reshape(parts, rows // parts, 2 * row_total)
    own_sum = lax.optimization_barrier(sum_blocks(products, MDL)).astype(jnp.bfloat16)
    lefts = gather_blocks(own_sum, MDL).reshape(rows, 2 * row_total)
    return lefts[:, :row_total], lefts[:, row_total:]


def cayley_own(mats, stack_a, stack_g):
    left_a, left_g = cayley_lefts(mats, stack_a, stack_g)
    partial = jnp.dot(left_a, stack_g, preferred_element_type=jnp.float32) - jnp.dot(
        left_g, stack_a, preferred_element_type=jnp.float32
    )
    partial = partial.astype(jnp.bfloat16)
    parts = lax.axis_size(TOK)
    return sum_blocks(partial.reshape(parts, -1, partial.shape[1]), TOK)


def gather_rotation(rot_b, line_wide, line_pos):
    near = lax.all_gather(rot_b, "ring", axis=0, tiled=True)
    others = jnp.stack([pick_other(k, line_wide, line_pos) for k in range(LINE - 1)])
    far = lax.all_gather(others, "ring", axis=1, tiled=True)
    thin = gather_blocks(near[:, :THIN], "line").reshape(LINE * near.shape[0], THIN)
    return thin, near, far


def pick_other(k, blocks, line_pos):
    return jnp.where(line_pos > k, blocks[k], blocks[k + 1])


def times_rotation(lhs, thin, near, far, line_pos):
    span = near.shape[0]
    spans = [lhs[:, k * span : (k + 1) * span] for k in range(LINE)]
    lhs_near = spans[LINE - 1]
    for k in range(LINE - 1):
        lhs_near = jnp.where(line_pos == k, spans[k], lhs_near)
    total_thin = jnp.dot(lhs, thin, preferred_element_type=jnp.float32)
    total = jnp.dot(lhs_near, near[:, THIN:], preferred_element_type=jnp.float32)
    for k in range(LINE - 1):
        total = total + jnp.dot(
            pick_other(k, spans, line_pos), far[k], preferred_element_type=jnp.float32
        )
    return jnp.concatenate([total_thin, total], 1)


def first_rows(thin, near, far, rows, line_pos):
    narrow = near.shape[1]
    first_near = near.reshape(RING, rows, narrow)[:, : 2 * WIN]
    first_far = far.reshape(LINE - 1, RING, rows, narrow - THIN)[:, :, : 2 * WIN]
    first_near, first_far = lax.optimization_barrier((first_near, first_far))
    first_near, first_far = first_near[:, :WIN, THIN:], first_far[:, :, :WIN]
    first = [
        jnp.where(
            line_pos == k,
            first_near,
            jnp.where(line_pos > k, first_far[min(k, LINE - 2)], first_far[max(k - 1, 0)]),
        )
        for k in range(LINE)
    ]
    first_thin = thin.reshape(LINE, RING, rows, THIN)[:, :, :WIN]
    return jnp.concatenate([first_thin, jnp.stack(first)], 3).reshape(LINE * RING * WIN, narrow)


def local(activations, rotation, value_weight, token_code, channel_code):
    n_tok = lax.axis_size(TOK)
    n_mdl = lax.axis_size(MDL)
    tok_pos = lax.axis_index(TOK)
    mdl_pos = lax.axis_index(MDL)
    narrow = rotation.shape[1]
    model_width = activations.shape[1]
    channels = value_weight.shape[1]
    chan_share = channels // n_tok
    tok_rows = activations.shape[0]
    width_root = math.sqrt(model_width)
    rot_b = rotation.astype(jnp.bfloat16)
    line_wide = gather_blocks(rot_b[:, THIN:], "line")
    value_late, line_wide = lax.optimization_barrier((value_weight, line_wide))
    own_cols = lax.dynamic_slice_in_dim(value_late, tok_pos * chan_share, chan_share, 1)
    weight_rows = gather_blocks(own_cols.T, MDL).transpose(1, 0, 2).reshape(chan_share, model_width)
    line_pos = lax.axis_index("line")
    panel = gather_rotation(rot_b, line_wide, line_pos)
    own_feats = lax.dynamic_slice_in_dim(activations, mdl_pos * narrow, narrow, 1)
    plain = jnp.dot(own_feats, value_weight, preferred_element_type=jnp.float32)

    turned = times_rotation(weight_rows, *panel, line_pos) / width_root
    own_codes = lax.dynamic_slice_in_dim(channel_code, tok_pos * chan_share, chan_share, 0)
    weight_clip = own_codes.astype(jnp.float32)[:, None] / (4.0 * width_root)
    weight_tanh = jnp.tanh(turned / weight_clip)
    quant_weight = (weight_clip * weight_tanh).astype(jnp.bfloat16)
    late_panel, quant_late = lax.optimization_barrier((panel, quant_weight))
    weight_full = gather_blocks(quant_late, TOK).reshape(channels, narrow)
    rotated = times_rotation(activations, *late_panel, line_pos) / width_root
    window = first_rows(*late_panel, rotation.shape[0], line_pos)
    act_clip = token_code.astype(jnp.float32)[:, None] * 0.5
    act_tanh = jnp.tanh(rotated / act_clip)
    quant_act = (act_clip * act_tanh).astype(jnp.bfloat16)
    half = channels // 2
    weight_halves = [weight_full[:half], weight_full[half:]]
    partial_err = jnp.stack(
        [
            jnp.einsum("td,cd->tc", quant_act, weight_half, preferred_element_type=jnp.float32)
            - plain_half
            for weight_half, plain_half in zip(weight_halves, (plain[:, :half], plain[:, half:]))
        ]
    )
    chips = lax.axis_size("chip")
    core_err = sum_blocks(partial_err, "core").reshape(chips, tok_rows // chips, half)
    core_err = gather_blocks(sum_blocks(core_err, "chip"), "chip").reshape(tok_rows, half)
    err_halves = gather_blocks(core_err, "core")
    recon_error = err_halves.transpose(1, 0, 2).reshape(tok_rows, channels)
    err_bf = err_halves.astype(jnp.bfloat16)
    grad_quant = sum_blocks(
        jnp.einsum("htc,td->hcd", err_bf, quant_act, preferred_element_type=jnp.float32)
        .astype(jnp.bfloat16)
        .reshape(n_tok, chan_share, narrow),
        TOK,
    )
    grad_act = sum(
        jnp.dot(err_half, weight_half, preferred_element_type=jnp.float32)
        for err_half, weight_half in zip(err_bf, weight_halves)
    )
    grad_act = (grad_act * (1.0 - act_tanh * act_tanh)).astype(jnp.bfloat16)
    grad_turned = (grad_quant * (1.0 - weight_tanh * weight_tanh)).astype(jnp.bfloat16)
    stack_a = jnp.concatenate([rotated.astype(jnp.bfloat16), turned.astype(jnp.bfloat16)], 0)
    stack_g = jnp.concatenate([grad_act, grad_turned], 0)
    step_size = STEP_GAIN / math.sqrt(tok_rows * n_tok * channels)
    own_rows = rotation[:WIN]
    moved = own_rows - step_size * cayley_own(window, stack_a, stack_g)
    second_in = gather_blocks((own_rows + moved).astype(jnp.bfloat16), TOK)
    second_in = second_in.reshape(n_tok * WIN, narrow)
    new_rows = own_rows - 0.5 * step_size * cayley_own(second_in, stack_a, stack_g)
    return (new_rows, recon_error)


def solution(mesh):
    mesh = Mesh(mesh.devices.reshape(LINE, RING, -1, 2), TOK + MDL)
    in_specs = (P(TOK, None), P(TOK, MDL), P(MDL, None), P(TOK), P())
    out_specs = (P(TOK, MDL), P(TOK, None))
    return jax.shard_map(local, mesh=mesh, in_specs=in_specs, out_specs=out_specs, check_vma=False)
```

```python
import math

import jax
import jax.numpy as jnp
from jax import lax
from jax.sharding import Mesh
from jax.sharding import PartitionSpec as P

WIN = 8


STEP_GAIN = 0.4

LINE, RING = 4, 8
TOK = ("line", "ring")
MDL = ("chip", "core")
THIN = 128


def gather_blocks(own, axis):
    parts = lax.axis_size(axis)
    return lax.all_to_all(jnp.broadcast_to(own[None], (parts,) + own.shape), axis, 0, 0)


def sum_blocks(blocks, axis):
    return jnp.sum(lax.all_to_all(blocks, axis, 0, 0).astype(jnp.float32), 0)


def cayley_lefts(mats, stack_a, stack_g):
    rows = mats.shape[0]
    row_total = stack_a.shape[0]
    parts = lax.axis_size(MDL)
    stacked = jnp.concatenate([stack_a, stack_g], 0)
    products = jnp.einsum("rd,kd->rk", mats, stacked, preferred_element_type=jnp.float32)
    products = products.astype(jnp.bfloat16).reshape(parts, rows // parts, 2 * row_total)
    own_sum = lax.optimization_barrier(sum_blocks(products, MDL)).astype(jnp.bfloat16)
    lefts = gather_blocks(own_sum, MDL).reshape(rows, 2 * row_total)
    return lefts[:, :row_total], lefts[:, row_total:]


def cayley_own(mats, stack_a, stack_g):
    left_a, left_g = cayley_lefts(mats, stack_a, stack_g)
    partial = jnp.dot(left_a, stack_g, preferred_element_type=jnp.float32) - jnp.dot(
        left_g, stack_a, preferred_element_type=jnp.float32
    )
    partial = partial.astype(jnp.bfloat16)
    parts = lax.axis_size(TOK)
    return sum_blocks(partial.reshape(parts, -1, partial.shape[1]), TOK)


def gather_rotation(rot_b, line_wide, line_pos):
    near = lax.all_gather(rot_b, "ring", axis=0, tiled=True)
    others = jnp.stack([pick_other(k, line_wide, line_pos) for k in range(LINE - 1)])
    far = lax.all_gather(others, "ring", axis=1, tiled=True)
    thin = gather_blocks(near[:, :THIN], "line").reshape(LINE * near.shape[0], THIN)
    return thin, near, far


def pick_other(k, blocks, line_pos):
    return jnp.where(line_pos > k, blocks[k], blocks[k + 1])


def times_rotation(lhs, thin, near, far, line_pos):
    span = near.shape[0]
    spans = [lhs[:, k * span : (k + 1) * span] for k in range(LINE)]
    lhs_near = spans[LINE - 1]
    for k in range(LINE - 1):
        lhs_near = jnp.where(line_pos == k, spans[k], lhs_near)
    total_thin = jnp.dot(lhs, thin, preferred_element_type=jnp.float32)
    total = jnp.dot(lhs_near, near[:, THIN:], preferred_element_type=jnp.float32)
    for k in range(LINE - 1):
        total = total + jnp.dot(
            pick_other(k, spans, line_pos), far[k], preferred_element_type=jnp.float32
        )
    return jnp.concatenate([total_thin, total], 1)


def first_rows(thin, near, far, rows, line_pos):
    narrow = near.shape[1]
    first_near = near.reshape(RING, rows, narrow)[:, : 2 * WIN]
    first_far = far.reshape(LINE - 1, RING, rows, narrow - THIN)[:, :, : 2 * WIN]
    first_near, first_far = lax.optimization_barrier((first_near, first_far))
    first_near, first_far = first_near[:, :WIN, THIN:], first_far[:, :, :WIN]
    first = [
        jnp.where(
            line_pos == k,
            first_near,
            jnp.where(line_pos > k, first_far[min(k, LINE - 2)], first_far[max(k - 1, 0)]),
        )
        for k in range(LINE)
    ]
    first_thin = thin.reshape(LINE, RING, rows, THIN)[:, :, :WIN]
    return jnp.concatenate([first_thin, jnp.stack(first)], 3).reshape(LINE * RING * WIN, narrow)


def local(activations, rotation, value_weight, token_code, channel_code):
    n_tok = lax.axis_size(TOK)
    n_mdl = lax.axis_size(MDL)
    tok_pos = lax.axis_index(TOK)
    mdl_pos = lax.axis_index(MDL)
    narrow = rotation.shape[1]
    model_width = activations.shape[1]
    channels = value_weight.shape[1]
    chan_share = channels // n_tok
    tok_rows = activations.shape[0]
    width_root = math.sqrt(model_width)
    rot_b = rotation.astype(jnp.bfloat16)
    line_wide = gather_blocks(rot_b[:, THIN:], "line")
    value_late, line_wide = lax.optimization_barrier((value_weight, line_wide))
    own_cols = lax.dynamic_slice_in_dim(value_late, tok_pos * chan_share, chan_share, 1)
    weight_rows = gather_blocks(own_cols.T, MDL).transpose(1, 0, 2).reshape(chan_share, model_width)
    line_pos = lax.axis_index("line")
    panel = gather_rotation(rot_b, line_wide, line_pos)
    own_feats = lax.dynamic_slice_in_dim(activations, mdl_pos * narrow, narrow, 1)
    plain = jnp.dot(own_feats, value_weight, preferred_element_type=jnp.float32)

    turned = times_rotation(weight_rows, *panel, line_pos) / width_root
    own_codes = lax.dynamic_slice_in_dim(channel_code, tok_pos * chan_share, chan_share, 0)
    weight_clip = own_codes.astype(jnp.float32)[:, None] / (4.0 * width_root)
    weight_tanh = jnp.tanh(turned / weight_clip)
    quant_weight = (weight_clip * weight_tanh).astype(jnp.bfloat16)
    late_panel, quant_late = lax.optimization_barrier((panel, quant_weight))
    weight_full = gather_blocks(quant_late, TOK).reshape(channels, narrow)
    rotated = times_rotation(activations, *late_panel, line_pos) / width_root
    window = first_rows(*late_panel, rotation.shape[0], line_pos)
    act_clip = token_code.astype(jnp.float32)[:, None] * 0.5
    act_tanh = jnp.tanh(rotated / act_clip)
    quant_act = (act_clip * act_tanh).astype(jnp.bfloat16)
    half = channels // 2
    weight_halves = weight_full.reshape(2, half, narrow)
    partial_err = (
        jnp.einsum("td,hcd->htc", quant_act, weight_halves, preferred_element_type=jnp.float32)
        - plain.reshape(tok_rows, 2, half).transpose(1, 0, 2)
    )
    own_err = sum_blocks(partial_err.reshape(n_mdl, -1, half), MDL)
    err_bf = gather_blocks(own_err.astype(jnp.bfloat16), MDL).reshape(2, tok_rows, half)
    recon_error = err_bf.transpose(1, 0, 2).reshape(tok_rows, channels).astype(jnp.float32)
    grad_quant = sum_blocks(
        jnp.einsum("htc,td->hcd", err_bf, quant_act, preferred_element_type=jnp.float32)
        .astype(jnp.bfloat16)
        .reshape(n_tok, chan_share, narrow),
        TOK,
    )
    grad_act = sum(
        jnp.dot(err_half, weight_half, preferred_element_type=jnp.float32)
        for err_half, weight_half in zip(err_bf, weight_halves)
    )
    grad_act = (grad_act * (1.0 - act_tanh * act_tanh)).astype(jnp.bfloat16)
    grad_turned = (grad_quant * (1.0 - weight_tanh * weight_tanh)).astype(jnp.bfloat16)
    stack_a = jnp.concatenate([rotated.astype(jnp.bfloat16), turned.astype(jnp.bfloat16)], 0)
    stack_g = jnp.concatenate([grad_act, grad_turned], 0)
    step_size = STEP_GAIN / math.sqrt(tok_rows * n_tok * channels)
    own_rows = rotation[:WIN]
    moved = own_rows - step_size * cayley_own(window, stack_a, stack_g)
    second_in = gather_blocks((own_rows + moved).astype(jnp.bfloat16), TOK)
    second_in = second_in.reshape(n_tok * WIN, narrow)
    new_rows = own_rows - 0.5 * step_size * cayley_own(second_in, stack_a, stack_g)
    return (new_rows, recon_error)


def solution(mesh):
    mesh = Mesh(mesh.devices.reshape(LINE, RING, -1, 2), TOK + MDL)
    in_specs = (P(TOK, None), P(TOK, MDL), P(MDL, None), P(TOK), P())
    out_specs = (P(TOK, MDL), P(TOK, None))
    return jax.shard_map(local, mesh=mesh, in_specs=in_specs, out_specs=out_specs, check_vma=False)
```

```python
import math

import jax
import jax.numpy as jnp
from jax import lax
from jax.sharding import Mesh
from jax.sharding import PartitionSpec as P

WIN = 8


STEP_GAIN = 0.4

LINE, RING = 4, 8
TOK = ("line", "ring")
MDL = ("chip", "core")
THIN = 128


def gather_blocks(own, axis):
    parts = lax.axis_size(axis)
    return lax.all_to_all(jnp.broadcast_to(own[None], (parts,) + own.shape), axis, 0, 0)


def sum_blocks(blocks, axis):
    return jnp.sum(lax.all_to_all(blocks, axis, 0, 0).astype(jnp.float32), 0)


def cayley_lefts(mats, stack_a, stack_g):
    rows = mats.shape[0]
    row_total = stack_a.shape[0]
    parts = lax.axis_size(MDL)
    stacked = jnp.concatenate([stack_a, stack_g], 0)
    products = jnp.einsum("rd,kd->rk", mats, stacked, preferred_element_type=jnp.float32)
    products = products.astype(jnp.bfloat16).reshape(parts, rows // parts, 2 * row_total)
    own_sum = lax.optimization_barrier(sum_blocks(products, MDL)).astype(jnp.bfloat16)
    lefts = gather_blocks(own_sum, MDL).reshape(rows, 2 * row_total)
    return lefts[:, :row_total], lefts[:, row_total:]


def cayley_own(mats, stack_a, stack_g):
    left_a, left_g = cayley_lefts(mats, stack_a, stack_g)
    partial = jnp.dot(left_a, stack_g, preferred_element_type=jnp.float32) - jnp.dot(
        left_g, stack_a, preferred_element_type=jnp.float32
    )
    partial = partial.astype(jnp.bfloat16)
    parts = lax.axis_size(TOK)
    return sum_blocks(partial.reshape(parts, -1, partial.shape[1]), TOK)


def gather_by_doubling(own):
    held = own[None]
    for axis in ("core", "chip"):
        size = lax.axis_size(axis)
        span = 1
        while span < size:
            came = lax.ppermute(held, axis, [(k, k ^ span) for k in range(size)])
            upper = (lax.axis_index(axis) // span) % 2 == 1
            held = jnp.concatenate(
                [jnp.where(upper, came, held), jnp.where(upper, held, came)], 0
            )
            span *= 2
    return held


def gather_rotation(rot_b):
    wide = gather_blocks(rot_b[:, THIN:], "line")
    thin_own, wide = lax.optimization_barrier((rot_b[:, :THIN], wide))
    thin = gather_blocks(thin_own, "ring").reshape(-1, THIN)
    wide = lax.all_gather(wide, "ring", axis=1, tiled=True)
    wide = wide.reshape(-1, wide.shape[2])
    return gather_blocks(thin, "line").reshape(-1, THIN), wide, thin


def times_rotation(lhs, thin, wide):
    return jnp.concatenate(
        [
            jnp.dot(lhs, thin, preferred_element_type=jnp.float32),
            jnp.dot(lhs, wide, preferred_element_type=jnp.float32),
        ],
        1,
    )


def first_rows(thin, wide, rows):
    firsts = [part.reshape(-1, rows, part.shape[1])[:, : 2 * WIN] for part in (thin, wide)]
    firsts = [part[:, :WIN] for part in lax.optimization_barrier(firsts)]
    return jnp.concatenate(firsts, 2).reshape(-1, thin.shape[1] + wide.shape[1])


def local(activations, rotation, value_weight, token_code, channel_code):
    n_tok = lax.axis_size(TOK)
    n_mdl = lax.axis_size(MDL)
    tok_pos = lax.axis_index(TOK)
    mdl_pos = lax.axis_index(MDL)
    narrow = rotation.shape[1]
    model_width = activations.shape[1]
    channels = value_weight.shape[1]
    chan_share = channels // n_tok
    tok_rows = activations.shape[0]
    width_root = math.sqrt(model_width)
    rot_b = rotation.astype(jnp.bfloat16)
    thin, wide, ring_thin = gather_rotation(rot_b)
    value_late, _ = lax.optimization_barrier((value_weight, ring_thin))
    own_cols = lax.dynamic_slice_in_dim(value_late, tok_pos * chan_share, chan_share, 1)
    weight_rows = gather_by_doubling(own_cols.T).transpose(1, 0, 2).reshape(chan_share, model_width)
    own_feats = lax.dynamic_slice_in_dim(activations, mdl_pos * narrow, narrow, 1)
    plain = jnp.dot(own_feats, value_weight, preferred_element_type=jnp.float32)

    turned = times_rotation(weight_rows, thin, wide) / width_root
    own_codes = lax.dynamic_slice_in_dim(channel_code, tok_pos * chan_share, chan_share, 0)
    weight_clip = own_codes.astype(jnp.float32)[:, None] / (4.0 * width_root)
    weight_tanh = jnp.tanh(turned / weight_clip)
    quant_weight = (weight_clip * weight_tanh).astype(jnp.bfloat16)
    thin, wide, quant_late = lax.optimization_barrier((thin, wide, quant_weight))
    weight_full = gather_blocks(quant_late, TOK).reshape(channels, narrow)
    rotated = times_rotation(activations, thin, wide) / width_root
    window = first_rows(thin, wide, rotation.shape[0])
    act_clip = token_code.astype(jnp.float32)[:, None] * 0.5
    act_tanh = jnp.tanh(rotated / act_clip)
    quant_act = (act_clip * act_tanh).astype(jnp.bfloat16)
    half = channels // 2
    weight_halves = weight_full.reshape(2, half, narrow)
    partial_err = (
        jnp.einsum("td,hcd->htc", quant_act, weight_halves, preferred_element_type=jnp.float32)
        - plain.reshape(tok_rows, 2, half).transpose(1, 0, 2)
    )
    own_err = sum_blocks(partial_err.reshape(n_mdl, -1, half), ("core", "chip"))
    err_bf = gather_blocks(own_err.astype(jnp.bfloat16), "chip").reshape(tok_rows, half)
    err_bf = gather_blocks(err_bf, "core")
    recon_error = err_bf.transpose(1, 0, 2).reshape(tok_rows, channels).astype(jnp.float32)
    grad_quant = sum_blocks(
        jnp.einsum("htc,td->hcd", err_bf, quant_act, preferred_element_type=jnp.float32)
        .astype(jnp.bfloat16)
        .reshape(n_tok, chan_share, narrow),
        TOK,
    )
    grad_act = sum(
        jnp.dot(err_half, weight_half, preferred_element_type=jnp.float32)
        for err_half, weight_half in zip(err_bf, weight_halves)
    )
    grad_act = (grad_act * (1.0 - act_tanh * act_tanh)).astype(jnp.bfloat16)
    grad_turned = (grad_quant * (1.0 - weight_tanh * weight_tanh)).astype(jnp.bfloat16)
    stack_a = jnp.concatenate([rotated.astype(jnp.bfloat16), turned.astype(jnp.bfloat16)], 0)
    stack_g = jnp.concatenate([grad_act, grad_turned], 0)
    step_size = STEP_GAIN / math.sqrt(tok_rows * n_tok * channels)
    own_rows = rotation[:WIN]
    moved = own_rows - step_size * cayley_own(window, stack_a, stack_g)
    second_in = gather_blocks((own_rows + moved).astype(jnp.bfloat16), TOK)
    second_in = second_in.reshape(n_tok * WIN, narrow)
    new_rows = own_rows - 0.5 * step_size * cayley_own(second_in, stack_a, stack_g)
    return (new_rows, recon_error)


def solution(mesh):
    mesh = Mesh(mesh.devices.reshape(LINE, RING, -1, 2), TOK + MDL)
    in_specs = (P(TOK, None), P(TOK, MDL), P(MDL, None), P(TOK), P())
    out_specs = (P(TOK, MDL), P(TOK, None))
    return jax.shard_map(local, mesh=mesh, in_specs=in_specs, out_specs=out_specs, check_vma=False)
```

```python
import math

import jax
import jax.numpy as jnp
from jax import lax
from jax.sharding import Mesh
from jax.sharding import PartitionSpec as P

WIN = 8


STEP_GAIN = 0.4

LINE, RING = 4, 8
TOK = ("line", "ring")
MDL = ("chip", "core")
THIN = 128
ERR_PARTS = 4


def gather_blocks(own, axis):
    parts = lax.axis_size(axis)
    return lax.all_to_all(jnp.broadcast_to(own[None], (parts,) + own.shape), axis, 0, 0)


def sum_blocks(blocks, axis):
    return jnp.sum(lax.all_to_all(blocks, axis, 0, 0).astype(jnp.float32), 0)


def cayley_lefts(mats, stack_a, stack_g):
    rows = mats.shape[0]
    row_total = stack_a.shape[0]
    parts = lax.axis_size(MDL)
    stacked = jnp.concatenate([stack_a, stack_g], 0)
    products = jnp.einsum("rd,kd->rk", mats, stacked, preferred_element_type=jnp.float32)
    products = products.astype(jnp.bfloat16).reshape(parts, rows // parts, 2 * row_total)
    own_sum = lax.optimization_barrier(sum_blocks(products, MDL)).astype(jnp.bfloat16)
    lefts = gather_blocks(own_sum, MDL).reshape(rows, 2 * row_total)
    return lefts[:, :row_total], lefts[:, row_total:]


def cayley_own(mats, stack_a, stack_g):
    left_a, left_g = cayley_lefts(mats, stack_a, stack_g)
    partial = jnp.dot(left_a, stack_g, preferred_element_type=jnp.float32) - jnp.dot(
        left_g, stack_a, preferred_element_type=jnp.float32
    )
    partial = partial.astype(jnp.bfloat16)
    parts = lax.axis_size(TOK)
    return sum_blocks(partial.reshape(parts, -1, partial.shape[1]), TOK)


def gather_rotation(rot_b, line_wide, line_pos):
    near = lax.all_gather(rot_b, "ring", axis=0, tiled=True)
    others = jnp.stack([pick_other(k, line_wide, line_pos) for k in range(LINE - 1)])
    far = lax.all_gather(others, "ring", axis=1, tiled=True)
    thin = gather_blocks(near[:, :THIN], "line").reshape(LINE * near.shape[0], THIN)
    return thin, near, far


def pick_other(k, blocks, line_pos):
    return jnp.where(line_pos > k, blocks[k], blocks[k + 1])


def times_rotation(lhs, thin, near, far, line_pos):
    span = near.shape[0]
    spans = [lhs[:, k * span : (k + 1) * span] for k in range(LINE)]
    lhs_near = spans[LINE - 1]
    for k in range(LINE - 1):
        lhs_near = jnp.where(line_pos == k, spans[k], lhs_near)
    total_thin = jnp.dot(lhs, thin, preferred_element_type=jnp.float32)
    total = jnp.dot(lhs_near, near[:, THIN:], preferred_element_type=jnp.float32)
    for k in range(LINE - 1):
        total = total + jnp.dot(
            pick_other(k, spans, line_pos), far[k], preferred_element_type=jnp.float32
        )
    return jnp.concatenate([total_thin, total], 1)


def first_rows(thin, near, far, rows, line_pos):
    narrow = near.shape[1]
    first_near = near.reshape(RING, rows, narrow)[:, : 2 * WIN]
    first_far = far.reshape(LINE - 1, RING, rows, narrow - THIN)[:, :, : 2 * WIN]
    first_near, first_far = lax.optimization_barrier((first_near, first_far))
    first_near, first_far = first_near[:, :WIN, THIN:], first_far[:, :, :WIN]
    first = [
        jnp.where(
            line_pos == k,
            first_near,
            jnp.where(line_pos > k, first_far[min(k, LINE - 2)], first_far[max(k - 1, 0)]),
        )
        for k in range(LINE)
    ]
    first_thin = thin.reshape(LINE, RING, rows, THIN)[:, :, :WIN]
    return jnp.concatenate([first_thin, jnp.stack(first)], 3).reshape(LINE * RING * WIN, narrow)


def local(activations, rotation, value_weight, token_code, channel_code):
    n_tok = lax.axis_size(TOK)
    n_mdl = lax.axis_size(MDL)
    tok_pos = lax.axis_index(TOK)
    mdl_pos = lax.axis_index(MDL)
    narrow = rotation.shape[1]
    model_width = activations.shape[1]
    channels = value_weight.shape[1]
    chan_share = channels // n_tok
    tok_rows = activations.shape[0]
    width_root = math.sqrt(model_width)
    rot_b = rotation.astype(jnp.bfloat16)
    line_wide = gather_blocks(rot_b[:, THIN:], "line")
    value_late, line_wide = lax.optimization_barrier((value_weight, line_wide))
    own_cols = lax.dynamic_slice_in_dim(value_late, tok_pos * chan_share, chan_share, 1)
    weight_rows = gather_blocks(own_cols.T, MDL).transpose(1, 0, 2).reshape(chan_share, model_width)
    line_pos = lax.axis_index("line")
    panel = gather_rotation(rot_b, line_wide, line_pos)
    own_feats = lax.dynamic_slice_in_dim(activations, mdl_pos * narrow, narrow, 1)
    plain = jnp.dot(own_feats, value_weight, preferred_element_type=jnp.float32)

    turned = times_rotation(weight_rows, *panel, line_pos) / width_root
    own_codes = lax.dynamic_slice_in_dim(channel_code, tok_pos * chan_share, chan_share, 0)
    weight_clip = own_codes.astype(jnp.float32)[:, None] / (4.0 * width_root)
    weight_tanh = jnp.tanh(turned / weight_clip)
    quant_weight = (weight_clip * weight_tanh).astype(jnp.bfloat16)
    late_panel, quant_late = lax.optimization_barrier((panel, quant_weight))
    weight_full = gather_blocks(quant_late, TOK).reshape(channels, narrow)
    rotated = times_rotation(activations, *late_panel, line_pos) / width_root
    window = first_rows(*late_panel, rotation.shape[0], line_pos)
    act_clip = token_code.astype(jnp.float32)[:, None] * 0.5
    act_tanh = jnp.tanh(rotated / act_clip)
    quant_act = (act_clip * act_tanh).astype(jnp.bfloat16)
    part = channels // ERR_PARTS
    weight_parts = weight_full.reshape(ERR_PARTS, part, narrow)
    partial_err = (
        jnp.einsum("td,hcd->htc", quant_act, weight_parts, preferred_element_type=jnp.float32)
        - plain.reshape(tok_rows, ERR_PARTS, part).transpose(1, 0, 2)
    )
    own_err = sum_blocks(partial_err.reshape(n_mdl, -1, part), MDL)
    err_bf = gather_blocks(own_err.astype(jnp.bfloat16), MDL).reshape(ERR_PARTS, tok_rows, part)
    recon_error = err_bf.transpose(1, 0, 2).reshape(tok_rows, channels).astype(jnp.float32)
    grad_quant = sum_blocks(
        jnp.einsum("htc,td->hcd", err_bf, quant_act, preferred_element_type=jnp.float32)
        .astype(jnp.bfloat16)
        .reshape(n_tok, chan_share, narrow),
        TOK,
    )
    grad_act = sum(
        jnp.dot(err_part, weight_part, preferred_element_type=jnp.float32)
        for err_part, weight_part in zip(err_bf, weight_parts)
    )
    grad_act = (grad_act * (1.0 - act_tanh * act_tanh)).astype(jnp.bfloat16)
    grad_turned = (grad_quant * (1.0 - weight_tanh * weight_tanh)).astype(jnp.bfloat16)
    stack_a = jnp.concatenate([rotated.astype(jnp.bfloat16), turned.astype(jnp.bfloat16)], 0)
    stack_g = jnp.concatenate([grad_act, grad_turned], 0)
    step_size = STEP_GAIN / math.sqrt(tok_rows * n_tok * channels)
    own_rows = rotation[:WIN]
    moved = own_rows - step_size * cayley_own(window, stack_a, stack_g)
    second_in = gather_blocks((own_rows + moved).astype(jnp.bfloat16), TOK)
    second_in = second_in.reshape(n_tok * WIN, narrow)
    new_rows = own_rows - 0.5 * step_size * cayley_own(second_in, stack_a, stack_g)
    return (new_rows, recon_error)


def solution(mesh):
    mesh = Mesh(mesh.devices.reshape(LINE, RING, -1, 2), TOK + MDL)
    in_specs = (P(TOK, None), P(TOK, MDL), P(MDL, None), P(TOK), P())
    out_specs = (P(TOK, MDL), P(TOK, None))
    return jax.shard_map(local, mesh=mesh, in_specs=in_specs, out_specs=out_specs, check_vma=False)
```

```python
import math

import jax
import jax.numpy as jnp
from jax import lax
from jax.sharding import Mesh
from jax.sharding import PartitionSpec as P

WIN = 8


STEP_GAIN = 0.4

LINE, RING = 4, 8
TOK = ("line", "ring")
MDL = ("chip", "core")
THIN = 128


def gather_blocks(own, axis):
    parts = lax.axis_size(axis)
    return lax.all_to_all(jnp.broadcast_to(own[None], (parts,) + own.shape), axis, 0, 0)


def sum_blocks(blocks, axis):
    return jnp.sum(lax.all_to_all(blocks, axis, 0, 0).astype(jnp.float32), 0)


def cayley_lefts(mats, stack_a, stack_g):
    rows = mats.shape[0]
    row_total = stack_a.shape[0]
    parts = lax.axis_size(MDL)
    stacked = jnp.concatenate([stack_a, stack_g], 0)
    products = jnp.einsum("rd,kd->rk", mats, stacked, preferred_element_type=jnp.float32)
    products = products.astype(jnp.bfloat16).reshape(parts, rows // parts, 2 * row_total)
    own_sum = lax.optimization_barrier(sum_blocks(products, MDL)).astype(jnp.bfloat16)
    lefts = gather_blocks(own_sum, MDL).reshape(rows, 2 * row_total)
    return lefts[:, :row_total], lefts[:, row_total:]


def cayley_own(mats, stack_a, stack_g):
    left_a, left_g = cayley_lefts(mats, stack_a, stack_g)
    partial = jnp.dot(left_a, stack_g, preferred_element_type=jnp.float32) - jnp.dot(
        left_g, stack_a, preferred_element_type=jnp.float32
    )
    partial = partial.astype(jnp.bfloat16)
    parts = lax.axis_size(TOK)
    return sum_blocks(partial.reshape(parts, -1, partial.shape[1]), TOK)


def gather_by_doubling(own):
    held = own[None]
    bits = 0
    for axis in MDL:
        size = lax.axis_size(axis)
        span = size // 2
        while span > 0:
            came = lax.ppermute(held, axis, [(k, k ^ span) for k in range(size)])
            upper = (lax.axis_index(axis) // span) % 2 == 1
            held = jnp.concatenate(
                [jnp.where(upper, came, held), jnp.where(upper, held, came)], 0
            )
            span //= 2
            bits += 1
    held = held.reshape((2,) * bits + own.shape)
    order = (bits,) + tuple(range(bits - 1, -1, -1)) + (bits + 1,)
    return held.transpose(order).reshape(own.shape[0], -1)


def gather_rotation(rot_b):
    wide = gather_blocks(rot_b[:, THIN:], "line")
    thin_own, wide = lax.optimization_barrier((rot_b[:, :THIN], wide))
    thin = gather_blocks(thin_own, "ring").reshape(-1, THIN)
    wide = lax.all_gather(wide, "ring", axis=1, tiled=True)
    wide = wide.reshape(-1, wide.shape[2])
    return gather_blocks(thin, "line").reshape(-1, THIN), wide, thin


def times_rotation(lhs, thin, wide):
    return jnp.concatenate(
        [
            jnp.dot(lhs, thin, preferred_element_type=jnp.float32),
            jnp.dot(lhs, wide, preferred_element_type=jnp.float32),
        ],
        1,
    )


def first_rows(thin, wide, rows):
    firsts = [part.reshape(-1, rows, part.shape[1])[:, : 2 * WIN] for part in (thin, wide)]
    firsts = [part[:, :WIN] for part in lax.optimization_barrier(firsts)]
    return jnp.concatenate(firsts, 2).reshape(-1, thin.shape[1] + wide.shape[1])


def local(activations, rotation, value_weight, token_code, channel_code):
    n_tok = lax.axis_size(TOK)
    n_mdl = lax.axis_size(MDL)
    tok_pos = lax.axis_index(TOK)
    mdl_pos = lax.axis_index(MDL)
    narrow = rotation.shape[1]
    model_width = activations.shape[1]
    channels = value_weight.shape[1]
    chan_share = channels // n_tok
    tok_rows = activations.shape[0]
    width_root = math.sqrt(model_width)
    rot_b = rotation.astype(jnp.bfloat16)
    thin, wide, ring_thin = gather_rotation(rot_b)
    value_late, _ = lax.optimization_barrier((value_weight, ring_thin))
    own_cols = lax.dynamic_slice_in_dim(value_late, tok_pos * chan_share, chan_share, 1)
    weight_rows = gather_by_doubling(own_cols.T)
    own_feats = lax.dynamic_slice_in_dim(activations, mdl_pos * narrow, narrow, 1)
    plain = jnp.dot(own_feats, value_weight, preferred_element_type=jnp.float32)

    turned = times_rotation(weight_rows, thin, wide) / width_root
    own_codes = lax.dynamic_slice_in_dim(channel_code, tok_pos * chan_share, chan_share, 0)
    weight_clip = own_codes.astype(jnp.float32)[:, None] / (4.0 * width_root)
    weight_tanh = jnp.tanh(turned / weight_clip)
    quant_weight = (weight_clip * weight_tanh).astype(jnp.bfloat16)
    thin, wide, quant_late = lax.optimization_barrier((thin, wide, quant_weight))
    weight_full = gather_blocks(quant_late, TOK).reshape(channels, narrow)
    rotated = times_rotation(activations, thin, wide) / width_root
    window = lax.optimization_barrier(first_rows(thin, wide, rotation.shape[0]))
    act_clip = token_code.astype(jnp.float32)[:, None] * 0.5
    act_tanh = jnp.tanh(rotated / act_clip)
    quant_act = (act_clip * act_tanh).astype(jnp.bfloat16)
    half = channels // 2
    weight_halves = weight_full.reshape(2, half, narrow)
    partial_err = (
        jnp.einsum("td,hcd->htc", quant_act, weight_halves, preferred_element_type=jnp.float32)
        - plain.reshape(tok_rows, 2, half).transpose(1, 0, 2)
    )
    core_err = sum_blocks(partial_err, "core")
    own_err = sum_blocks(core_err.reshape(lax.axis_size("chip"), -1, half), "chip")
    err_bf = gather_blocks(own_err.astype(jnp.bfloat16), ("core", "chip")).reshape(2, tok_rows, half)
    recon_error = err_bf.transpose(1, 0, 2).reshape(tok_rows, channels).astype(jnp.float32)
    grad_quant = sum_blocks(
        jnp.einsum("htc,td->hcd", err_bf, quant_act, preferred_element_type=jnp.float32)
        .astype(jnp.bfloat16)
        .reshape(n_tok, chan_share, narrow),
        TOK,
    )
    grad_act = sum(
        jnp.dot(err_half, weight_half, preferred_element_type=jnp.float32)
        for err_half, weight_half in zip(err_bf, weight_halves)
    )
    grad_act = (grad_act * (1.0 - act_tanh * act_tanh)).astype(jnp.bfloat16)
    grad_turned = (grad_quant * (1.0 - weight_tanh * weight_tanh)).astype(jnp.bfloat16)
    stack_a = jnp.concatenate([rotated.astype(jnp.bfloat16), turned.astype(jnp.bfloat16)], 0)
    stack_g = jnp.concatenate([grad_act, grad_turned], 0)
    step_size = STEP_GAIN / math.sqrt(tok_rows * n_tok * channels)
    own_rows = rotation[:WIN]
    moved = own_rows - step_size * cayley_own(window, stack_a, stack_g)
    second_in = gather_blocks((own_rows + moved).astype(jnp.bfloat16), TOK)
    second_in = second_in.reshape(n_tok * WIN, narrow)
    new_rows = own_rows - 0.5 * step_size * cayley_own(second_in, stack_a, stack_g)
    return (new_rows, recon_error)


def solution(mesh):
    mesh = Mesh(mesh.devices.reshape(LINE, RING, -1, 2), TOK + MDL)
    in_specs = (P(TOK, None), P(TOK, MDL), P(MDL, None), P(TOK), P())
    out_specs = (P(TOK, MDL), P(TOK, None))
    return jax.shard_map(local, mesh=mesh, in_specs=in_specs, out_specs=out_specs, check_vma=False)
```

```python
import math

import jax
import jax.numpy as jnp
from jax import lax
from jax.sharding import Mesh
from jax.sharding import PartitionSpec as P

WIN = 8


STEP_GAIN = 0.4

LINE, RING = 4, 8
TOK = ("line", "ring")
MDL = ("chip", "core")
THIN = 128


def gather_blocks(own, axis):
    parts = lax.axis_size(axis)
    return lax.all_to_all(jnp.broadcast_to(own[None], (parts,) + own.shape), axis, 0, 0)


def sum_blocks(blocks, axis):
    return jnp.sum(lax.all_to_all(blocks, axis, 0, 0).astype(jnp.float32), 0)


def cayley_lefts(mats, stack_a, stack_g):
    rows = mats.shape[0]
    row_total = stack_a.shape[0]
    parts = lax.axis_size(MDL)
    stacked = jnp.concatenate([stack_a, stack_g], 0)
    products = jnp.einsum("rd,kd->rk", mats, stacked, preferred_element_type=jnp.float32)
    products = products.astype(jnp.bfloat16).reshape(parts, rows // parts, 2 * row_total)
    own_sum = lax.optimization_barrier(sum_blocks(products, MDL)).astype(jnp.bfloat16)
    lefts = gather_blocks(own_sum, MDL).reshape(rows, 2 * row_total)
    return lefts[:, :row_total], lefts[:, row_total:]


def cayley_own(mats, stack_a, stack_g):
    left_a, left_g = cayley_lefts(mats, stack_a, stack_g)
    partial = jnp.dot(left_a, stack_g, preferred_element_type=jnp.float32) - jnp.dot(
        left_g, stack_a, preferred_element_type=jnp.float32
    )
    partial = partial.astype(jnp.bfloat16)
    parts = lax.axis_size(TOK)
    return sum_blocks(partial.reshape(parts, -1, partial.shape[1]), TOK)


def gather_rotation(rot_b, line_wide, line_pos):
    near = lax.all_gather(rot_b, "ring", axis=0, tiled=True)
    others = jnp.stack([pick_other(k, line_wide, line_pos) for k in range(LINE - 1)])
    far = lax.all_gather(others, "ring", axis=1, tiled=True)
    thin = gather_blocks(near[:, :THIN], "line").reshape(LINE * near.shape[0], THIN)
    return thin, near, far


def pick_other(k, blocks, line_pos):
    return jnp.where(line_pos > k, blocks[k], blocks[k + 1])


def times_rotation(lhs, thin, near, far, line_pos):
    span = near.shape[0]
    spans = [lhs[:, k * span : (k + 1) * span] for k in range(LINE)]
    lhs_near = spans[LINE - 1]
    for k in range(LINE - 1):
        lhs_near = jnp.where(line_pos == k, spans[k], lhs_near)
    total_thin = jnp.dot(lhs, thin, preferred_element_type=jnp.float32)
    total = jnp.dot(lhs_near, near[:, THIN:], preferred_element_type=jnp.float32)
    for k in range(LINE - 1):
        total = total + jnp.dot(
            pick_other(k, spans, line_pos), far[k], preferred_element_type=jnp.float32
        )
    return jnp.concatenate([total_thin, total], 1)


def first_rows(thin, near, far, rows, line_pos):
    narrow = near.shape[1]
    first_near = near.reshape(RING, rows, narrow)[:, : 2 * WIN]
    first_far = far.reshape(LINE - 1, RING, rows, narrow - THIN)[:, :, : 2 * WIN]
    first_near, first_far = lax.optimization_barrier((first_near, first_far))
    first_near, first_far = first_near[:, :WIN, THIN:], first_far[:, :, :WIN]
    first = [
        jnp.where(
            line_pos == k,
            first_near,
            jnp.where(line_pos > k, first_far[min(k, LINE - 2)], first_far[max(k - 1, 0)]),
        )
        for k in range(LINE)
    ]
    first_thin = thin.reshape(LINE, RING, rows, THIN)[:, :, :WIN]
    return jnp.concatenate([first_thin, jnp.stack(first)], 3).reshape(LINE * RING * WIN, narrow)


def local(activations, rotation, value_weight, token_code, channel_code):
    n_tok = lax.axis_size(TOK)
    n_mdl = lax.axis_size(MDL)
    tok_pos = lax.axis_index(TOK)
    mdl_pos = lax.axis_index(MDL)
    narrow = rotation.shape[1]
    model_width = activations.shape[1]
    channels = value_weight.shape[1]
    chan_share = channels // n_tok
    tok_rows = activations.shape[0]
    width_root = math.sqrt(model_width)
    rot_b = rotation.astype(jnp.bfloat16)
    line_wide = gather_blocks(rot_b[:, THIN:], "line")
    value_late, line_wide = lax.optimization_barrier((value_weight, line_wide))
    own_cols = lax.dynamic_slice_in_dim(value_late, tok_pos * chan_share, chan_share, 1)
    weight_rows = gather_blocks(own_cols.T, MDL).transpose(1, 0, 2).reshape(chan_share, model_width)
    line_pos = lax.axis_index("line")
    panel = gather_rotation(rot_b, line_wide, line_pos)
    own_feats = lax.dynamic_slice_in_dim(activations, mdl_pos * narrow, narrow, 1)
    plain = jnp.dot(own_feats, value_weight, preferred_element_type=jnp.float32)

    turned = times_rotation(weight_rows, *panel, line_pos) / width_root
    own_codes = lax.dynamic_slice_in_dim(channel_code, tok_pos * chan_share, chan_share, 0)
    weight_clip = own_codes.astype(jnp.float32)[:, None] / (4.0 * width_root)
    weight_tanh = jnp.tanh(turned / weight_clip)
    quant_weight = (weight_clip * weight_tanh).astype(jnp.bfloat16)
    late_panel, quant_late = lax.optimization_barrier((panel, quant_weight))
    weight_full = gather_blocks(quant_late, TOK).reshape(channels, narrow)
    rotated = times_rotation(activations, *late_panel, line_pos) / width_root
    window = first_rows(*late_panel, rotation.shape[0], line_pos)
    act_clip = token_code.astype(jnp.float32)[:, None] * 0.5
    act_tanh = jnp.tanh(rotated / act_clip)
    quant_act = (act_clip * act_tanh).astype(jnp.bfloat16)
    half = channels // 2
    weight_halves = weight_full.reshape(2, half, narrow)
    partial_err = (
        jnp.einsum("td,hcd->htc", quant_act, weight_halves, preferred_element_type=jnp.float32)
        - plain.reshape(tok_rows, 2, half).transpose(1, 0, 2)
    )
    core_err = sum_blocks(partial_err, "core")
    own_err = sum_blocks(core_err.reshape(lax.axis_size("chip"), -1, half), "chip")
    err_bf = gather_blocks(own_err.astype(jnp.bfloat16), ("core", "chip")).reshape(2, tok_rows, half)
    recon_error = err_bf.transpose(1, 0, 2).reshape(tok_rows, channels).astype(jnp.float32)
    grad_quant = sum_blocks(
        jnp.einsum("htc,td->hcd", err_bf, quant_act, preferred_element_type=jnp.float32)
        .astype(jnp.bfloat16)
        .reshape(n_tok, chan_share, narrow),
        TOK,
    )
    grad_act = sum(
        jnp.dot(err_half, weight_half, preferred_element_type=jnp.float32)
        for err_half, weight_half in zip(err_bf, weight_halves)
    )
    grad_act = (grad_act * (1.0 - act_tanh * act_tanh)).astype(jnp.bfloat16)
    grad_turned = (grad_quant * (1.0 - weight_tanh * weight_tanh)).astype(jnp.bfloat16)
    stack_a = jnp.concatenate([rotated.astype(jnp.bfloat16), turned.astype(jnp.bfloat16)], 0)
    stack_g = jnp.concatenate([grad_act, grad_turned], 0)
    step_size = STEP_GAIN / math.sqrt(tok_rows * n_tok * channels)
    own_rows = rotation[:WIN]
    moved = own_rows - step_size * cayley_own(window, stack_a, stack_g)
    second_in = gather_blocks((own_rows + moved).astype(jnp.bfloat16), TOK)
    second_in = second_in.reshape(n_tok * WIN, narrow)
    new_rows = own_rows - 0.5 * step_size * cayley_own(second_in, stack_a, stack_g)
    return (new_rows, recon_error)


def solution(mesh):
    mesh = Mesh(mesh.devices.reshape(LINE, RING, -1, 2), TOK + MDL)
    in_specs = (P(TOK, None), P(TOK, MDL), P(MDL, None), P(TOK), P())
    out_specs = (P(TOK, MDL), P(TOK, None))
    return jax.shard_map(local, mesh=mesh, in_specs=in_specs, out_specs=out_specs, check_vma=False)
```

```python
import math

import jax
import jax.numpy as jnp
from jax import lax
from jax.sharding import Mesh
from jax.sharding import PartitionSpec as P

WIN = 8


STEP_GAIN = 0.4

LINE, RING = 4, 8
TOK = ("line", "ring")
MDL = ("chip", "core")
THIN = 128


def gather_blocks(own, axis):
    parts = lax.axis_size(axis)
    return lax.all_to_all(jnp.broadcast_to(own[None], (parts,) + own.shape), axis, 0, 0)


def sum_blocks(blocks, axis):
    return jnp.sum(lax.all_to_all(blocks, axis, 0, 0).astype(jnp.float32), 0)


def cayley_lefts(mats, stack_a, stack_g):
    rows = mats.shape[0]
    row_total = stack_a.shape[0]
    parts = lax.axis_size(MDL)
    stacked = jnp.concatenate([stack_a, stack_g], 0)
    products = jnp.einsum("rd,kd->rk", mats, stacked, preferred_element_type=jnp.float32)
    products = products.astype(jnp.bfloat16).reshape(parts, rows // parts, 2 * row_total)
    own_sum = lax.optimization_barrier(sum_blocks(products, MDL)).astype(jnp.bfloat16)
    lefts = gather_blocks(own_sum, MDL).reshape(rows, 2 * row_total)
    return lefts[:, :row_total], lefts[:, row_total:]


def cayley_own(mats, stack_a, stack_g):
    left_a, left_g = cayley_lefts(mats, stack_a, stack_g)
    partial = jnp.dot(left_a, stack_g, preferred_element_type=jnp.float32) - jnp.dot(
        left_g, stack_a, preferred_element_type=jnp.float32
    )
    partial = partial.astype(jnp.bfloat16)
    parts = lax.axis_size(TOK)
    return sum_blocks(partial.reshape(parts, -1, partial.shape[1]), TOK)


def gather_rotation(rot_b, line_wide, line_pos):
    near = lax.all_gather(rot_b, "ring", axis=0, tiled=True)
    others = jnp.stack([pick_other(k, line_wide, line_pos) for k in range(LINE - 1)])
    far = lax.all_gather(others, "ring", axis=1, tiled=True)
    thin = gather_blocks(near[:, :THIN], "line").reshape(LINE * near.shape[0], THIN)
    return thin, near, far


def pick_other(k, blocks, line_pos):
    return jnp.where(line_pos > k, blocks[k], blocks[k + 1])


def times_rotation(lhs, thin, near, far, line_pos):
    span = near.shape[0]
    spans = [lhs[:, k * span : (k + 1) * span] for k in range(LINE)]
    lhs_near = spans[LINE - 1]
    for k in range(LINE - 1):
        lhs_near = jnp.where(line_pos == k, spans[k], lhs_near)
    lhs_far = jnp.concatenate([pick_other(k, spans, line_pos) for k in range(LINE - 1)], 1)
    total_thin = jnp.dot(lhs, thin, preferred_element_type=jnp.float32)
    total_near = jnp.dot(lhs_near, near[:, THIN:], preferred_element_type=jnp.float32)
    lhs_far, total_near = lax.optimization_barrier((lhs_far, total_near))
    total = total_near + jnp.dot(
        lhs_far, far.reshape(lhs_far.shape[1], -1), preferred_element_type=jnp.float32
    )
    return jnp.concatenate([total_thin, total], 1)


def first_rows(thin, near, far, rows, line_pos):
    narrow = near.shape[1]
    first_near = near.reshape(RING, rows, narrow)[:, : 2 * WIN]
    first_far = far.reshape(LINE - 1, RING, rows, narrow - THIN)[:, :, : 2 * WIN]
    first_near, first_far = lax.optimization_barrier((first_near, first_far))
    first_near, first_far = first_near[:, :WIN, THIN:], first_far[:, :, :WIN]
    first = [
        jnp.where(
            line_pos == k,
            first_near,
            jnp.where(line_pos > k, first_far[min(k, LINE - 2)], first_far[max(k - 1, 0)]),
        )
        for k in range(LINE)
    ]
    first_thin = thin.reshape(LINE, RING, rows, THIN)[:, :, :WIN]
    return jnp.concatenate([first_thin, jnp.stack(first)], 3).reshape(LINE * RING * WIN, narrow)


def local(activations, rotation, value_weight, token_code, channel_code):
    n_tok = lax.axis_size(TOK)
    n_mdl = lax.axis_size(MDL)
    tok_pos = lax.axis_index(TOK)
    mdl_pos = lax.axis_index(MDL)
    narrow = rotation.shape[1]
    model_width = activations.shape[1]
    channels = value_weight.shape[1]
    chan_share = channels // n_tok
    tok_rows = activations.shape[0]
    width_root = math.sqrt(model_width)
    rot_b = rotation.astype(jnp.bfloat16)
    line_wide = gather_blocks(rot_b[:, THIN:], "line")
    value_late, line_wide = lax.optimization_barrier((value_weight, line_wide))
    own_cols = lax.dynamic_slice_in_dim(value_late, tok_pos * chan_share, chan_share, 1)
    weight_rows = gather_blocks(own_cols.T, MDL).transpose(1, 0, 2).reshape(chan_share, model_width)
    line_pos = lax.axis_index("line")
    panel = gather_rotation(rot_b, line_wide, line_pos)
    own_feats = lax.dynamic_slice_in_dim(activations, mdl_pos * narrow, narrow, 1)
    plain = jnp.dot(own_feats, value_weight, preferred_element_type=jnp.float32)
    plain = plain.reshape(tok_rows, 2, channels // 2).transpose(1, 0, 2)

    turned = times_rotation(weight_rows, *panel, line_pos) / width_root
    own_codes = lax.dynamic_slice_in_dim(channel_code, tok_pos * chan_share, chan_share, 0)
    weight_clip = own_codes.astype(jnp.float32)[:, None] / (4.0 * width_root)
    weight_tanh = jnp.tanh(turned / weight_clip)
    quant_weight = (weight_clip * weight_tanh).astype(jnp.bfloat16)
    late_panel, quant_late = lax.optimization_barrier((panel, quant_weight))
    weight_full = gather_blocks(quant_late, TOK).reshape(channels, narrow)
    rotated = times_rotation(activations, *late_panel, line_pos) / width_root
    window = first_rows(*late_panel, rotation.shape[0], line_pos)
    act_clip = token_code.astype(jnp.float32)[:, None] * 0.5
    act_tanh = jnp.tanh(rotated / act_clip)
    quant_act = (act_clip * act_tanh).astype(jnp.bfloat16)
    half = channels // 2
    core_pos = lax.axis_index("core")
    weight_parts = weight_full.reshape(2, half, narrow)
    terms = []
    for part in (1 - core_pos, core_pos):
        product = jnp.einsum(
            "td,cd->tc",
            quant_act,
            lax.dynamic_index_in_dim(weight_parts, part, 0, keepdims=False),
            preferred_element_type=jnp.float32,
        )
        terms.append(product - lax.dynamic_index_in_dim(plain, part, 0, keepdims=False))
    core_err = terms[1] + lax.ppermute(terms[0], "core", [(0, 1), (1, 0)])
    own_err = sum_blocks(core_err.reshape(lax.axis_size("chip"), -1, half), "chip")
    err_bf = gather_blocks(own_err.astype(jnp.bfloat16), ("core", "chip")).reshape(2, tok_rows, half)
    recon_error = err_bf.transpose(1, 0, 2).reshape(tok_rows, channels).astype(jnp.float32)
    grad_quant = sum_blocks(
        jnp.einsum("htc,td->hcd", err_bf, quant_act, preferred_element_type=jnp.float32)
        .astype(jnp.bfloat16)
        .reshape(n_tok, chan_share, narrow),
        TOK,
    )
    grad_act = sum(
        jnp.dot(err_half, weight_half, preferred_element_type=jnp.float32)
        for err_half, weight_half in zip(err_bf, weight_parts)
    )
    grad_act = (grad_act * (1.0 - act_tanh * act_tanh)).astype(jnp.bfloat16)
    grad_turned = (grad_quant * (1.0 - weight_tanh * weight_tanh)).astype(jnp.bfloat16)
    stack_a = jnp.concatenate([rotated.astype(jnp.bfloat16), turned.astype(jnp.bfloat16)], 0)
    stack_g = jnp.concatenate([grad_act, grad_turned], 0)
    step_size = STEP_GAIN / math.sqrt(tok_rows * n_tok * channels)
    own_rows = rotation[:WIN]
    moved = own_rows - step_size * cayley_own(window, stack_a, stack_g)
    second_in = gather_blocks((own_rows + moved).astype(jnp.bfloat16), TOK)
    second_in = second_in.reshape(n_tok * WIN, narrow)
    new_rows = own_rows - 0.5 * step_size * cayley_own(second_in, stack_a, stack_g)
    return (new_rows, recon_error)


def solution(mesh):
    mesh = Mesh(mesh.devices.reshape(LINE, RING, -1, 2), TOK + MDL)
    in_specs = (P(TOK, None), P(TOK, MDL), P(MDL, None), P(TOK), P())
    out_specs = (P(TOK, MDL), P(TOK, None))
    return jax.shard_map(local, mesh=mesh, in_specs=in_specs, out_specs=out_specs, check_vma=False)
```

```python
import math

import jax
import jax.numpy as jnp
from jax import lax
from jax.sharding import Mesh
from jax.sharding import PartitionSpec as P

WIN = 8


STEP_GAIN = 0.4

LINE, RING = 4, 8
TOK = ("line", "ring")
MDL = ("chip", "core")
THIN = 128


def gather_blocks(own, axis):
    parts = lax.axis_size(axis)
    return lax.all_to_all(jnp.broadcast_to(own[None], (parts,) + own.shape), axis, 0, 0)


def sum_blocks(blocks, axis):
    return jnp.sum(lax.all_to_all(blocks, axis, 0, 0).astype(jnp.float32), 0)


def cayley_lefts(mats, stack_a, stack_g):
    rows = mats.shape[0]
    row_total = stack_a.shape[0]
    parts = lax.axis_size(MDL)
    stacked = jnp.concatenate([stack_a, stack_g], 0)
    products = jnp.einsum("rd,kd->rk", mats, stacked, preferred_element_type=jnp.float32)
    products = products.astype(jnp.bfloat16).reshape(parts, rows // parts, 2 * row_total)
    own_sum = lax.optimization_barrier(sum_blocks(products, MDL)).astype(jnp.bfloat16)
    lefts = gather_blocks(own_sum, MDL).reshape(rows, 2 * row_total)
    return lefts[:, :row_total], lefts[:, row_total:]


def cayley_own(mats, stack_a, stack_g):
    left_a, left_g = cayley_lefts(mats, stack_a, stack_g)
    partial = jnp.dot(left_a, stack_g, preferred_element_type=jnp.float32) - jnp.dot(
        left_g, stack_a, preferred_element_type=jnp.float32
    )
    partial = partial.astype(jnp.bfloat16)
    parts = lax.axis_size(TOK)
    return sum_blocks(partial.reshape(parts, -1, partial.shape[1]), TOK)


def gather_rotation(rot_b, line_wide, line_pos):
    near = lax.all_gather(rot_b, "ring", axis=0, tiled=True)
    others = jnp.stack([pick_other(k, line_wide, line_pos) for k in range(LINE - 1)])
    far = lax.all_gather(others, "ring", axis=1, tiled=True)
    thin = gather_blocks(near[:, :THIN], "line").reshape(LINE * near.shape[0], THIN)
    return thin, near, far


def pick_other(k, blocks, line_pos):
    return jnp.where(line_pos > k, blocks[k], blocks[k + 1])


def times_rotation(lhs, thin, near, far, line_pos):
    span = near.shape[0]
    spans = [lhs[:, k * span : (k + 1) * span] for k in range(LINE)]
    lhs_near = spans[LINE - 1]
    for k in range(LINE - 1):
        lhs_near = jnp.where(line_pos == k, spans[k], lhs_near)
    lhs_far = jnp.concatenate([pick_other(k, spans, line_pos) for k in range(LINE - 1)], 1)
    total_thin = jnp.dot(lhs, thin, preferred_element_type=jnp.float32)
    total_near = jnp.dot(lhs_near, near[:, THIN:], preferred_element_type=jnp.float32)
    lhs_far, total_near = lax.optimization_barrier((lhs_far, total_near))
    total = total_near + jnp.dot(
        lhs_far, far.reshape(lhs_far.shape[1], -1), preferred_element_type=jnp.float32
    )
    return jnp.concatenate([total_thin, total], 1)


def first_rows(thin, near, far, rows, line_pos):
    narrow = near.shape[1]
    first_near = near.reshape(RING, rows, narrow)[:, : 2 * WIN]
    first_far = far.reshape(LINE - 1, RING, rows, narrow - THIN)[:, :, : 2 * WIN]
    first_near, first_far = lax.optimization_barrier((first_near, first_far))
    first_near, first_far = first_near[:, :WIN, THIN:], first_far[:, :, :WIN]
    first = [
        jnp.where(
            line_pos == k,
            first_near,
            jnp.where(line_pos > k, first_far[min(k, LINE - 2)], first_far[max(k - 1, 0)]),
        )
        for k in range(LINE)
    ]
    first_thin = thin.reshape(LINE, RING, rows, THIN)[:, :, :WIN]
    return jnp.concatenate([first_thin, jnp.stack(first)], 3).reshape(LINE * RING * WIN, narrow)


def local(activations, rotation, value_weight, token_code, channel_code):
    n_tok = lax.axis_size(TOK)
    n_mdl = lax.axis_size(MDL)
    tok_pos = lax.axis_index(TOK)
    mdl_pos = lax.axis_index(MDL)
    narrow = rotation.shape[1]
    model_width = activations.shape[1]
    channels = value_weight.shape[1]
    chan_share = channels // n_tok
    tok_rows = activations.shape[0]
    width_root = math.sqrt(model_width)
    rot_b = rotation.astype(jnp.bfloat16)
    line_wide = gather_blocks(rot_b[:, THIN:], "line")
    value_late, line_wide = lax.optimization_barrier((value_weight, line_wide))
    own_cols = lax.dynamic_slice_in_dim(value_late, tok_pos * chan_share, chan_share, 1)
    core_pos = lax.axis_index("core")
    chip_rows = gather_blocks(own_cols.T, "chip")
    pair_rows = lax.ppermute(chip_rows, "core", [(0, 1), (1, 0)])
    weight_rows = jnp.stack(
        [
            jnp.where(core_pos == 0, chip_rows, pair_rows),
            jnp.where(core_pos == 0, pair_rows, chip_rows),
        ],
        1,
    )
    weight_rows = weight_rows.transpose(2, 0, 1, 3).reshape(chan_share, model_width)
    line_pos = lax.axis_index("line")
    panel = gather_rotation(rot_b, line_wide, line_pos)
    own_feats = lax.dynamic_slice_in_dim(activations, mdl_pos * narrow, narrow, 1)
    plain = jnp.dot(own_feats, value_weight, preferred_element_type=jnp.float32)
    plain = plain.reshape(tok_rows, 2, channels // 2).transpose(1, 0, 2)

    turned = times_rotation(weight_rows, *panel, line_pos) / width_root
    own_codes = lax.dynamic_slice_in_dim(channel_code, tok_pos * chan_share, chan_share, 0)
    weight_clip = own_codes.astype(jnp.float32)[:, None] / (4.0 * width_root)
    weight_tanh = jnp.tanh(turned / weight_clip)
    quant_weight = (weight_clip * weight_tanh).astype(jnp.bfloat16)
    late_panel, quant_late = lax.optimization_barrier((panel, quant_weight))
    weight_full = gather_blocks(quant_late, TOK).reshape(channels, narrow)
    rotated = times_rotation(activations, *late_panel, line_pos) / width_root
    window = first_rows(*late_panel, rotation.shape[0], line_pos)
    act_clip = token_code.astype(jnp.float32)[:, None] * 0.5
    act_tanh = jnp.tanh(rotated / act_clip)
    quant_act = (act_clip * act_tanh).astype(jnp.bfloat16)
    half = channels // 2
    weight_parts = weight_full.reshape(2, half, narrow)
    terms = []
    for part in (1 - core_pos, core_pos):
        product = jnp.einsum(
            "td,cd->tc",
            quant_act,
            lax.dynamic_index_in_dim(weight_parts, part, 0, keepdims=False),
            preferred_element_type=jnp.float32,
        )
        terms.append(product - lax.dynamic_index_in_dim(plain, part, 0, keepdims=False))
    core_err = terms[1] + lax.ppermute(terms[0], "core", [(0, 1), (1, 0)])
    own_err = sum_blocks(core_err.reshape(lax.axis_size("chip"), -1, half), "chip")
    err_bf = gather_blocks(own_err.astype(jnp.bfloat16), ("core", "chip")).reshape(2, tok_rows, half)
    recon_error = err_bf.transpose(1, 0, 2).reshape(tok_rows, channels).astype(jnp.float32)
    grad_quant = sum_blocks(
        jnp.einsum("htc,td->hcd", err_bf, quant_act, preferred_element_type=jnp.float32)
        .astype(jnp.bfloat16)
        .reshape(n_tok, chan_share, narrow),
        TOK,
    )
    grad_act = sum(
        jnp.dot(err_half, weight_half, preferred_element_type=jnp.float32)
        for err_half, weight_half in zip(err_bf, weight_parts)
    )
    grad_act = (grad_act * (1.0 - act_tanh * act_tanh)).astype(jnp.bfloat16)
    grad_turned = (grad_quant * (1.0 - weight_tanh * weight_tanh)).astype(jnp.bfloat16)
    stack_a = jnp.concatenate([rotated.astype(jnp.bfloat16), turned.astype(jnp.bfloat16)], 0)
    stack_g = jnp.concatenate([grad_act, grad_turned], 0)
    step_size = STEP_GAIN / math.sqrt(tok_rows * n_tok * channels)
    own_rows = rotation[:WIN]
    moved = own_rows - step_size * cayley_own(window, stack_a, stack_g)
    second_in = gather_blocks((own_rows + moved).astype(jnp.bfloat16), TOK)
    second_in = second_in.reshape(n_tok * WIN, narrow)
    new_rows = own_rows - 0.5 * step_size * cayley_own(second_in, stack_a, stack_g)
    return (new_rows, recon_error)


def solution(mesh):
    mesh = Mesh(mesh.devices.reshape(LINE, RING, -1, 2), TOK + MDL)
    in_specs = (P(TOK, None), P(TOK, MDL), P(MDL, None), P(TOK), P())
    out_specs = (P(TOK, MDL), P(TOK, None))
    return jax.shard_map(local, mesh=mesh, in_specs=in_specs, out_specs=out_specs, check_vma=False)
```

```python
import math

import jax
import jax.numpy as jnp
from jax import lax
from jax.sharding import Mesh
from jax.sharding import PartitionSpec as P

WIN = 8


STEP_GAIN = 0.4

LINE, RING = 4, 8
TOK = ("line", "ring")
MDL = ("chip", "core")
THIN = 128


def gather_blocks(own, axis):
    parts = lax.axis_size(axis)
    return lax.all_to_all(jnp.broadcast_to(own[None], (parts,) + own.shape), axis, 0, 0)


def sum_blocks(blocks, axis):
    return jnp.sum(lax.all_to_all(blocks, axis, 0, 0).astype(jnp.float32), 0)


def cayley_lefts(mats, stack_a, stack_g):
    rows = mats.shape[0]
    row_total = stack_a.shape[0]
    parts = lax.axis_size(MDL)
    stacked = jnp.concatenate([stack_a, stack_g], 0)
    products = jnp.einsum("rd,kd->rk", mats, stacked, preferred_element_type=jnp.float32)
    products = products.astype(jnp.bfloat16).reshape(parts, rows // parts, 2 * row_total)
    own_sum = lax.optimization_barrier(sum_blocks(products, MDL)).astype(jnp.bfloat16)
    lefts = gather_blocks(own_sum, MDL).reshape(rows, 2 * row_total)
    return lefts[:, :row_total], lefts[:, row_total:]


def cayley_own(mats, stack_a, stack_g):
    left_a, left_g = cayley_lefts(mats, stack_a, stack_g)
    partial = jnp.dot(left_a, stack_g, preferred_element_type=jnp.float32) - jnp.dot(
        left_g, stack_a, preferred_element_type=jnp.float32
    )
    partial = partial.astype(jnp.bfloat16)
    parts = lax.axis_size(TOK)
    return sum_blocks(partial.reshape(parts, -1, partial.shape[1]), TOK)


def gather_rotation(rot_b, line_wide, line_pos):
    near = lax.all_gather(rot_b, "ring", axis=0, tiled=True)
    others = jnp.stack([pick_other(k, line_wide, line_pos) for k in range(LINE - 1)])
    middle = ring_pass(others[:, :, :THIN])
    far = lax.all_gather(others[:, :, THIN:], "ring", axis=1, tiled=True)
    thin = gather_blocks(near[:, :THIN], "line").reshape(LINE * near.shape[0], THIN)
    return thin, near, middle, far


def ring_pass(own):
    up = [(k, (k + 1) % RING) for k in range(RING)]
    down = [(k, (k - 1) % RING) for k in range(RING)]
    found = {0: own}
    for step in range(1, RING // 2 + 1):
        found[RING - step] = lax.ppermute(found[(RING - step + 1) % RING], "ring", up)
        if step < RING // 2:
            found[step] = lax.ppermute(found[step - 1], "ring", down)
    near_first = [found[k] for k in range(RING)]
    twice = jnp.stack(near_first + near_first, 1)
    start = (RING - lax.axis_index("ring")) % RING
    ordered = lax.dynamic_slice_in_dim(twice, start, RING, 1)
    return ordered.reshape(own.shape[0], -1, own.shape[2])


def pick_other(k, blocks, line_pos):
    return jnp.where(line_pos > k, blocks[k], blocks[k + 1])


def times_rotation(lhs, thin, near, middle, far, line_pos):
    span = near.shape[0]
    spans = [lhs[:, k * span : (k + 1) * span] for k in range(LINE)]
    lhs_near = spans[LINE - 1]
    for k in range(LINE - 1):
        lhs_near = jnp.where(line_pos == k, spans[k], lhs_near)
    lhs_far = jnp.concatenate([pick_other(k, spans, line_pos) for k in range(LINE - 1)], 1)
    total_thin = jnp.dot(lhs, thin, preferred_element_type=jnp.float32)
    total_near = jnp.dot(lhs_near, near[:, THIN:], preferred_element_type=jnp.float32)
    total_mid = total_near[:, :THIN] + jnp.dot(
        lhs_far, middle.reshape(lhs_far.shape[1], -1), preferred_element_type=jnp.float32
    )
    lhs_far, total_near, total_mid = lax.optimization_barrier(
        (lhs_far, total_near[:, THIN:], total_mid)
    )
    total = total_near + jnp.dot(
        lhs_far, far.reshape(lhs_far.shape[1], -1), preferred_element_type=jnp.float32
    )
    return jnp.concatenate([total_thin, total_mid, total], 1)


def first_rows(thin, near, middle, far, rows, line_pos):
    narrow = near.shape[1]
    first_near = near.reshape(RING, rows, narrow)[:, : 2 * WIN]
    first_far = [
        part.reshape(LINE - 1, RING, rows, -1)[:, :, : 2 * WIN] for part in (middle, far)
    ]
    first_near, first_far = lax.optimization_barrier((first_near, first_far))
    first_near = first_near[:, :WIN, THIN:]
    first_far = jnp.concatenate([part[:, :, :WIN] for part in first_far], 3)
    first = [
        jnp.where(
            line_pos == k,
            first_near,
            jnp.where(line_pos > k, first_far[min(k, LINE - 2)], first_far[max(k - 1, 0)]),
        )
        for k in range(LINE)
    ]
    first_thin = thin.reshape(LINE, RING, rows, THIN)[:, :, :WIN]
    return jnp.concatenate([first_thin, jnp.stack(first)], 3).reshape(LINE * RING * WIN, narrow)


def local(activations, rotation, value_weight, token_code, channel_code):
    n_tok = lax.axis_size(TOK)
    n_mdl = lax.axis_size(MDL)
    tok_pos = lax.axis_index(TOK)
    mdl_pos = lax.axis_index(MDL)
    narrow = rotation.shape[1]
    model_width = activations.shape[1]
    channels = value_weight.shape[1]
    chan_share = channels // n_tok
    tok_rows = activations.shape[0]
    width_root = math.sqrt(model_width)
    rot_b = rotation.astype(jnp.bfloat16)
    line_wide = gather_blocks(rot_b[:, THIN:], "line")
    value_late, line_wide = lax.optimization_barrier((value_weight, line_wide))
    own_cols = lax.dynamic_slice_in_dim(value_late, tok_pos * chan_share, chan_share, 1)
    core_pos = lax.axis_index("core")
    chip_rows = gather_blocks(own_cols.T, "chip")
    pair_rows = lax.ppermute(chip_rows, "core", [(0, 1), (1, 0)])
    weight_rows = jnp.stack(
        [
            jnp.where(core_pos == 0, chip_rows, pair_rows),
            jnp.where(core_pos == 0, pair_rows, chip_rows),
        ],
        1,
    )
    weight_rows = weight_rows.transpose(2, 0, 1, 3).reshape(chan_share, model_width)
    line_pos = lax.axis_index("line")
    panel = gather_rotation(rot_b, line_wide, line_pos)
    own_feats = lax.dynamic_slice_in_dim(activations, mdl_pos * narrow, narrow, 1)
    plain = jnp.dot(own_feats, value_weight, preferred_element_type=jnp.float32)
    plain = plain.reshape(tok_rows, 2, channels // 2).transpose(1, 0, 2)

    turned = times_rotation(weight_rows, *panel, line_pos) / width_root
    own_codes = lax.dynamic_slice_in_dim(channel_code, tok_pos * chan_share, chan_share, 0)
    weight_clip = own_codes.astype(jnp.float32)[:, None] / (4.0 * width_root)
    weight_tanh = jnp.tanh(turned / weight_clip)
    quant_weight = (weight_clip * weight_tanh).astype(jnp.bfloat16)
    late_panel, quant_late = lax.optimization_barrier((panel, quant_weight))
    weight_full = gather_blocks(quant_late, TOK).reshape(channels, narrow)
    rotated = times_rotation(activations, *late_panel, line_pos) / width_root
    window = first_rows(*late_panel, rotation.shape[0], line_pos)
    act_clip = token_code.astype(jnp.float32)[:, None] * 0.5
    act_tanh = jnp.tanh(rotated / act_clip)
    quant_act = (act_clip * act_tanh).astype(jnp.bfloat16)
    half = channels // 2
    weight_parts = weight_full.reshape(2, half, narrow)
    terms = []
    for part in (1 - core_pos, core_pos):
        product = jnp.einsum(
            "td,cd->tc",
            quant_act,
            lax.dynamic_index_in_dim(weight_parts, part, 0, keepdims=False),
            preferred_element_type=jnp.float32,
        )
        terms.append(product - lax.dynamic_index_in_dim(plain, part, 0, keepdims=False))
    core_err = terms[1] + lax.ppermute(terms[0], "core", [(0, 1), (1, 0)])
    own_err = sum_blocks(core_err.reshape(lax.axis_size("chip"), -1, half), "chip")
    err_bf = gather_blocks(own_err.astype(jnp.bfloat16), ("core", "chip")).reshape(2, tok_rows, half)
    recon_error = err_bf.transpose(1, 0, 2).reshape(tok_rows, channels).astype(jnp.float32)
    grad_quant = sum_blocks(
        jnp.einsum("htc,td->hcd", err_bf, quant_act, preferred_element_type=jnp.float32)
        .astype(jnp.bfloat16)
        .reshape(n_tok, chan_share, narrow),
        TOK,
    )
    grad_act = sum(
        jnp.dot(err_half, weight_half, preferred_element_type=jnp.float32)
        for err_half, weight_half in zip(err_bf, weight_parts)
    )
    grad_act = (grad_act * (1.0 - act_tanh * act_tanh)).astype(jnp.bfloat16)
    grad_turned = (grad_quant * (1.0 - weight_tanh * weight_tanh)).astype(jnp.bfloat16)
    stack_a = jnp.concatenate([rotated.astype(jnp.bfloat16), turned.astype(jnp.bfloat16)], 0)
    stack_g = jnp.concatenate([grad_act, grad_turned], 0)
    step_size = STEP_GAIN / math.sqrt(tok_rows * n_tok * channels)
    own_rows = rotation[:WIN]
    moved = own_rows - step_size * cayley_own(window, stack_a, stack_g)
    second_in = gather_blocks((own_rows + moved).astype(jnp.bfloat16), TOK)
    second_in = second_in.reshape(n_tok * WIN, narrow)
    new_rows = own_rows - 0.5 * step_size * cayley_own(second_in, stack_a, stack_g)
    return (new_rows, recon_error)


def solution(mesh):
    mesh = Mesh(mesh.devices.reshape(LINE, RING, -1, 2), TOK + MDL)
    in_specs = (P(TOK, None), P(TOK, MDL), P(MDL, None), P(TOK), P())
    out_specs = (P(TOK, MDL), P(TOK, None))
    return jax.shard_map(local, mesh=mesh, in_specs=in_specs, out_specs=out_specs, check_vma=False)
```

```python
import math

import jax
import jax.numpy as jnp
from jax import lax
from jax.sharding import Mesh
from jax.sharding import PartitionSpec as P

WIN = 8


STEP_GAIN = 0.4

LINE, RING = 4, 8
TOK = ("line", "ring")
MDL = ("chip", "core")
THIN = 128


def gather_blocks(own, axis):
    parts = lax.axis_size(axis)
    return lax.all_to_all(jnp.broadcast_to(own[None], (parts,) + own.shape), axis, 0, 0)


def sum_blocks(blocks, axis):
    return jnp.sum(lax.all_to_all(blocks, axis, 0, 0).astype(jnp.float32), 0)


def cayley_lefts(mats, stack_a, stack_g):
    rows = mats.shape[0]
    row_total = stack_a.shape[0]
    parts = lax.axis_size(MDL)
    stacked = jnp.concatenate([stack_a, stack_g], 0)
    products = jnp.einsum("rd,kd->rk", mats, stacked, preferred_element_type=jnp.float32)
    products = products.astype(jnp.bfloat16).reshape(parts, rows // parts, 2 * row_total)
    own_sum = lax.optimization_barrier(sum_blocks(products, MDL)).astype(jnp.bfloat16)
    lefts = gather_blocks(own_sum, MDL).reshape(rows, 2 * row_total)
    return lefts[:, :row_total], lefts[:, row_total:]


def cayley_own(mats, stack_a, stack_g):
    left_a, left_g = cayley_lefts(mats, stack_a, stack_g)
    partial = jnp.dot(left_a, stack_g, preferred_element_type=jnp.float32) - jnp.dot(
        left_g, stack_a, preferred_element_type=jnp.float32
    )
    partial = partial.astype(jnp.bfloat16)
    parts = lax.axis_size(TOK)
    return sum_blocks(partial.reshape(parts, -1, partial.shape[1]), TOK)


def gather_rotation(rot_b, line_wide, line_pos):
    near = lax.all_gather(rot_b, "ring", axis=0, tiled=True)
    others = jnp.stack([pick_other(k, line_wide, line_pos) for k in range(LINE - 1)])
    far = lax.all_gather(others[:, :, THIN:], "ring", axis=1, tiled=True)
    thin_own, middle_own = lax.optimization_barrier((near[:, :THIN], others[:, :, :THIN]))
    thin = gather_blocks(thin_own, "line").reshape(LINE * near.shape[0], THIN)
    return thin, near, ring_pass(middle_own), far


def ring_pass(own):
    up = [(k, (k + 1) % RING) for k in range(RING)]
    down = [(k, (k - 1) % RING) for k in range(RING)]
    found = {0: own}
    for step in range(1, RING // 2 + 1):
        found[RING - step] = lax.ppermute(found[(RING - step + 1) % RING], "ring", up)
        if step < RING // 2:
            found[step] = lax.ppermute(found[step - 1], "ring", down)
    ordered = jnp.zeros((own.shape[0], RING) + own.shape[1:], own.dtype)
    for k in range(RING):
        place = (lax.axis_index("ring") + k) % RING
        ordered = lax.dynamic_update_index_in_dim(ordered, found[k], place, 1)
    return ordered.reshape(own.shape[0], -1, own.shape[2])


def pick_other(k, blocks, line_pos):
    return jnp.where(line_pos > k, blocks[k], blocks[k + 1])


def times_rotation(lhs, thin, near, middle, far, line_pos):
    span = near.shape[0]
    spans = [lhs[:, k * span : (k + 1) * span] for k in range(LINE)]
    lhs_near = spans[LINE - 1]
    for k in range(LINE - 1):
        lhs_near = jnp.where(line_pos == k, spans[k], lhs_near)
    lhs_far = jnp.concatenate([pick_other(k, spans, line_pos) for k in range(LINE - 1)], 1)
    total_thin = jnp.dot(lhs, thin, preferred_element_type=jnp.float32)
    total_near = jnp.dot(lhs_near, near[:, THIN:], preferred_element_type=jnp.float32)
    total_mid = total_near[:, :THIN] + jnp.dot(
        lhs_far, middle.reshape(lhs_far.shape[1], -1), preferred_element_type=jnp.float32
    )
    lhs_far, total_near, total_mid = lax.optimization_barrier(
        (lhs_far, total_near[:, THIN:], total_mid)
    )
    total = total_near + jnp.dot(
        lhs_far, far.reshape(lhs_far.shape[1], -1), preferred_element_type=jnp.float32
    )
    return jnp.concatenate([total_thin, total_mid, total], 1)


def first_rows(thin, near, middle, far, rows, line_pos):
    narrow = near.shape[1]
    first_near = near.reshape(RING, rows, narrow)[:, : 2 * WIN]
    first_far = [
        part.reshape(LINE - 1, RING, rows, -1)[:, :, : 2 * WIN] for part in (middle, far)
    ]
    first_near, first_far = lax.optimization_barrier((first_near, first_far))
    first_near = first_near[:, :WIN, THIN:]
    first_far = jnp.concatenate([part[:, :, :WIN] for part in first_far], 3)
    first = [
        jnp.where(
            line_pos == k,
            first_near,
            jnp.where(line_pos > k, first_far[min(k, LINE - 2)], first_far[max(k - 1, 0)]),
        )
        for k in range(LINE)
    ]
    first_thin = thin.reshape(LINE, RING, rows, THIN)[:, :, :WIN]
    return jnp.concatenate([first_thin, jnp.stack(first)], 3).reshape(LINE * RING * WIN, narrow)


def local(activations, rotation, value_weight, token_code, channel_code):
    n_tok = lax.axis_size(TOK)
    n_mdl = lax.axis_size(MDL)
    tok_pos = lax.axis_index(TOK)
    mdl_pos = lax.axis_index(MDL)
    narrow = rotation.shape[1]
    model_width = activations.shape[1]
    channels = value_weight.shape[1]
    chan_share = channels // n_tok
    tok_rows = activations.shape[0]
    width_root = math.sqrt(model_width)
    rot_b = rotation.astype(jnp.bfloat16)
    line_wide = gather_blocks(rot_b[:, THIN:], "line")
    value_late, line_wide = lax.optimization_barrier((value_weight, line_wide))
    own_cols = lax.dynamic_slice_in_dim(value_late, tok_pos * chan_share, chan_share, 1)
    core_pos = lax.axis_index("core")
    chip_rows = gather_blocks(own_cols.T, "chip")
    pair_rows = lax.ppermute(chip_rows, "core", [(0, 1), (1, 0)])
    weight_rows = jnp.stack(
        [
            jnp.where(core_pos == 0, chip_rows, pair_rows),
            jnp.where(core_pos == 0, pair_rows, chip_rows),
        ],
        1,
    )
    weight_rows = weight_rows.transpose(2, 0, 1, 3).reshape(chan_share, model_width)
    line_pos = lax.axis_index("line")
    panel = gather_rotation(rot_b, line_wide, line_pos)
    own_feats = lax.dynamic_slice_in_dim(activations, mdl_pos * narrow, narrow, 1)
    plain = jnp.dot(own_feats, value_weight, preferred_element_type=jnp.float32)
    plain = plain.reshape(tok_rows, 2, channels // 2).transpose(1, 0, 2)

    turned = times_rotation(weight_rows, *panel, line_pos) / width_root
    own_codes = lax.dynamic_slice_in_dim(channel_code, tok_pos * chan_share, chan_share, 0)
    weight_clip = own_codes.astype(jnp.float32)[:, None] / (4.0 * width_root)
    weight_tanh = jnp.tanh(turned / weight_clip)
    quant_weight = (weight_clip * weight_tanh).astype(jnp.bfloat16)
    late_panel, quant_late = lax.optimization_barrier((panel, quant_weight))
    weight_full = gather_blocks(quant_late, TOK).reshape(channels, narrow)
    rotated = times_rotation(activations, *late_panel, line_pos) / width_root
    window = first_rows(*late_panel, rotation.shape[0], line_pos)
    act_clip = token_code.astype(jnp.float32)[:, None] * 0.5
    act_tanh = jnp.tanh(rotated / act_clip)
    quant_act = (act_clip * act_tanh).astype(jnp.bfloat16)
    half = channels // 2
    weight_parts = weight_full.reshape(2, half, narrow)
    terms = []
    for part in (1 - core_pos, core_pos):
        product = jnp.einsum(
            "td,cd->tc",
            quant_act,
            lax.dynamic_index_in_dim(weight_parts, part, 0, keepdims=False),
            preferred_element_type=jnp.float32,
        )
        terms.append(product - lax.dynamic_index_in_dim(plain, part, 0, keepdims=False))
    core_err = terms[1] + lax.ppermute(terms[0], "core", [(0, 1), (1, 0)])
    own_err = sum_blocks(core_err.reshape(lax.axis_size("chip"), -1, half), "chip")
    err_bf = gather_blocks(own_err.astype(jnp.bfloat16), ("core", "chip")).reshape(2, tok_rows, half)
    recon_error = err_bf.transpose(1, 0, 2).reshape(tok_rows, channels).astype(jnp.float32)
    grad_quant = sum_blocks(
        jnp.einsum("htc,td->hcd", err_bf, quant_act, preferred_element_type=jnp.float32)
        .astype(jnp.bfloat16)
        .reshape(n_tok, chan_share, narrow),
        TOK,
    )
    grad_act = sum(
        jnp.dot(err_half, weight_half, preferred_element_type=jnp.float32)
        for err_half, weight_half in zip(err_bf, weight_parts)
    )
    grad_act = (grad_act * (1.0 - act_tanh * act_tanh)).astype(jnp.bfloat16)
    grad_turned = (grad_quant * (1.0 - weight_tanh * weight_tanh)).astype(jnp.bfloat16)
    stack_a = jnp.concatenate([rotated.astype(jnp.bfloat16), turned.astype(jnp.bfloat16)], 0)
    stack_g = jnp.concatenate([grad_act, grad_turned], 0)
    step_size = STEP_GAIN / math.sqrt(tok_rows * n_tok * channels)
    own_rows = rotation[:WIN]
    moved = own_rows - step_size * cayley_own(window, stack_a, stack_g)
    second_in = gather_blocks((own_rows + moved).astype(jnp.bfloat16), TOK)
    second_in = second_in.reshape(n_tok * WIN, narrow)
    new_rows = own_rows - 0.5 * step_size * cayley_own(second_in, stack_a, stack_g)
    return (new_rows, recon_error)


def solution(mesh):
    mesh = Mesh(mesh.devices.reshape(LINE, RING, -1, 2), TOK + MDL)
    in_specs = (P(TOK, None), P(TOK, MDL), P(MDL, None), P(TOK), P())
    out_specs = (P(TOK, MDL), P(TOK, None))
    return jax.shard_map(local, mesh=mesh, in_specs=in_specs, out_specs=out_specs, check_vma=False)
```

```python
import math

import jax
import jax.numpy as jnp
from jax import lax
from jax.sharding import Mesh
from jax.sharding import PartitionSpec as P

WIN = 8


STEP_GAIN = 0.4

LINE, RING = 4, 8
TOK = ("line", "ring")
MDL = ("chip", "core")
THIN = 128


def gather_blocks(own, axis):
    parts = lax.axis_size(axis)
    return lax.all_to_all(jnp.broadcast_to(own[None], (parts,) + own.shape), axis, 0, 0)


def sum_blocks(blocks, axis):
    return jnp.sum(lax.all_to_all(blocks, axis, 0, 0).astype(jnp.float32), 0)


def cayley_lefts(mats, stack_a, stack_g):
    rows = mats.shape[0]
    row_total = stack_a.shape[0]
    parts = lax.axis_size(MDL)
    stacked = jnp.concatenate([stack_a, stack_g], 0)
    products = jnp.einsum("rd,kd->rk", mats, stacked, preferred_element_type=jnp.float32)
    products = products.astype(jnp.bfloat16).reshape(parts, rows // parts, 2 * row_total)
    own_sum = lax.optimization_barrier(sum_blocks(products, MDL)).astype(jnp.bfloat16)
    lefts = gather_blocks(own_sum, MDL).reshape(rows, 2 * row_total)
    return lefts[:, :row_total], lefts[:, row_total:]


def cayley_own(mats, stack_a, stack_g):
    left_a, left_g = cayley_lefts(mats, stack_a, stack_g)
    partial = jnp.dot(left_a, stack_g, preferred_element_type=jnp.float32) - jnp.dot(
        left_g, stack_a, preferred_element_type=jnp.float32
    )
    partial = partial.astype(jnp.bfloat16)
    parts = lax.axis_size(TOK)
    return sum_blocks(partial.reshape(parts, -1, partial.shape[1]), TOK)


def gather_rotation(rot_b, line_wide, line_pos):
    near = lax.all_gather(rot_b, "ring", axis=0, tiled=True)
    others = jnp.stack([pick_other(k, line_wide, line_pos) for k in range(LINE - 1)])
    far = lax.all_gather(others, "ring", axis=1, tiled=True)
    thin = gather_blocks(near[:, :THIN], "line").reshape(LINE * near.shape[0], THIN)
    return thin, near, far


def pick_other(k, blocks, line_pos):
    return jnp.where(line_pos > k, blocks[k], blocks[k + 1])


def times_rotation(lhs, thin, near, far, line_pos):
    span = near.shape[0]
    spans = [lhs[:, k * span : (k + 1) * span] for k in range(LINE)]
    lhs_near = spans[LINE - 1]
    for k in range(LINE - 1):
        lhs_near = jnp.where(line_pos == k, spans[k], lhs_near)
    lhs_far = jnp.concatenate([pick_other(k, spans, line_pos) for k in range(LINE - 1)], 1)
    total_thin = jnp.dot(lhs, thin, preferred_element_type=jnp.float32)
    total_near = jnp.dot(lhs_near, near[:, THIN:], preferred_element_type=jnp.float32)
    lhs_far, total_near = lax.optimization_barrier((lhs_far, total_near))
    total = total_near + jnp.dot(
        lhs_far, far.reshape(lhs_far.shape[1], -1), preferred_element_type=jnp.float32
    )
    return jnp.concatenate([total_thin, total], 1)


def first_rows(thin, near, far, rows, line_pos):
    narrow = near.shape[1]
    first_near = near.reshape(RING, rows, narrow)[:, : 2 * WIN]
    first_far = far.reshape(LINE - 1, RING, rows, narrow - THIN)[:, :, : 2 * WIN]
    first_near, first_far = lax.optimization_barrier((first_near, first_far))
    first_near, first_far = first_near[:, :WIN, THIN:], first_far[:, :, :WIN]
    first = [
        jnp.where(
            line_pos == k,
            first_near,
            jnp.where(line_pos > k, first_far[min(k, LINE - 2)], first_far[max(k - 1, 0)]),
        )
        for k in range(LINE)
    ]
    first_thin = thin.reshape(LINE, RING, rows, THIN)[:, :, :WIN]
    return jnp.concatenate([first_thin, jnp.stack(first)], 3).reshape(LINE * RING * WIN, narrow)


def local(activations, rotation, value_weight, token_code, channel_code):
    n_tok = lax.axis_size(TOK)
    n_mdl = lax.axis_size(MDL)
    tok_pos = lax.axis_index(TOK)
    mdl_pos = lax.axis_index(MDL)
    narrow = rotation.shape[1]
    model_width = activations.shape[1]
    channels = value_weight.shape[1]
    chan_share = channels // n_tok
    tok_rows = activations.shape[0]
    width_root = math.sqrt(model_width)
    rot_b = rotation.astype(jnp.bfloat16)
    line_wide = gather_blocks(rot_b[:, THIN:], "line")
    value_late, line_wide = lax.optimization_barrier((value_weight, line_wide))
    own_cols = lax.dynamic_slice_in_dim(value_late, tok_pos * chan_share, chan_share, 1)
    core_pos = lax.axis_index("core")
    chip_rows = gather_blocks(own_cols.T, "chip")
    pair_rows = lax.ppermute(chip_rows, "core", [(0, 1), (1, 0)])
    weight_rows = jnp.stack(
        [
            jnp.where(core_pos == 0, chip_rows, pair_rows),
            jnp.where(core_pos == 0, pair_rows, chip_rows),
        ],
        1,
    )
    weight_rows = weight_rows.transpose(2, 0, 1, 3).reshape(chan_share, model_width)
    line_pos = lax.axis_index("line")
    panel = gather_rotation(rot_b, line_wide, line_pos)
    own_feats = lax.dynamic_slice_in_dim(activations, mdl_pos * narrow, narrow, 1)
    plain = jnp.dot(own_feats, value_weight, preferred_element_type=jnp.float32)
    plain = plain.reshape(tok_rows, 2, channels // 2).transpose(1, 0, 2)

    turned = times_rotation(weight_rows, *panel, line_pos) / width_root
    own_codes = lax.dynamic_slice_in_dim(channel_code, tok_pos * chan_share, chan_share, 0)
    weight_clip = own_codes.astype(jnp.float32)[:, None] / (4.0 * width_root)
    weight_tanh = jnp.tanh(turned / weight_clip)
    quant_weight = (weight_clip * weight_tanh).astype(jnp.bfloat16)
    late_panel, quant_late = lax.optimization_barrier((panel, quant_weight))
    weight_full = gather_blocks(quant_late, TOK).reshape(channels, narrow)
    rotated = times_rotation(activations, *late_panel, line_pos) / width_root
    window = first_rows(*late_panel, rotation.shape[0], line_pos)
    act_clip = token_code.astype(jnp.float32)[:, None] * 0.5
    act_tanh = jnp.tanh(rotated / act_clip)
    quant_act = (act_clip * act_tanh).astype(jnp.bfloat16)
    half = channels // 2
    weight_parts = weight_full.reshape(2, half, narrow)
    terms = []
    for part in (1 - core_pos, core_pos):
        product = jnp.einsum(
            "td,cd->tc",
            quant_act,
            lax.dynamic_index_in_dim(weight_parts, part, 0, keepdims=False),
            preferred_element_type=jnp.float32,
        )
        terms.append(product - lax.dynamic_index_in_dim(plain, part, 0, keepdims=False))
    core_err = lax.optimization_barrier(terms[1])
    core_err = core_err + lax.ppermute(terms[0], "core", [(0, 1), (1, 0)])
    own_err = sum_blocks(core_err.reshape(lax.axis_size("chip"), -1, half), "chip")
    err_bf = gather_blocks(own_err.astype(jnp.bfloat16), ("core", "chip")).reshape(2, tok_rows, half)
    recon_error = err_bf.transpose(1, 0, 2).reshape(tok_rows, channels).astype(jnp.float32)
    grad_quant = sum_blocks(
        jnp.einsum("htc,td->hcd", err_bf, quant_act, preferred_element_type=jnp.float32)
        .astype(jnp.bfloat16)
        .reshape(n_tok, chan_share, narrow),
        TOK,
    )
    grad_act = sum(
        jnp.dot(err_half, weight_half, preferred_element_type=jnp.float32)
        for err_half, weight_half in zip(err_bf, weight_parts)
    )
    grad_act = (grad_act * (1.0 - act_tanh * act_tanh)).astype(jnp.bfloat16)
    grad_turned = (grad_quant * (1.0 - weight_tanh * weight_tanh)).astype(jnp.bfloat16)
    stack_a = jnp.concatenate([rotated.astype(jnp.bfloat16), turned.astype(jnp.bfloat16)], 0)
    stack_g = jnp.concatenate([grad_act, grad_turned], 0)
    step_size = STEP_GAIN / math.sqrt(tok_rows * n_tok * channels)
    own_rows = rotation[:WIN]
    moved = own_rows - step_size * cayley_own(window, stack_a, stack_g)
    second_in = gather_blocks((own_rows + moved).astype(jnp.bfloat16), TOK)
    second_in = second_in.reshape(n_tok * WIN, narrow)
    new_rows = own_rows - 0.5 * step_size * cayley_own(second_in, stack_a, stack_g)
    return (new_rows, recon_error)


def solution(mesh):
    mesh = Mesh(mesh.devices.reshape(LINE, RING, -1, 2), TOK + MDL)
    in_specs = (P(TOK, None), P(TOK, MDL), P(MDL, None), P(TOK), P())
    out_specs = (P(TOK, MDL), P(TOK, None))
    return jax.shard_map(local, mesh=mesh, in_specs=in_specs, out_specs=out_specs, check_vma=False)
```
